32 devices in a mesh: replica: 16 (over z, y, x), tensor: 2 (over core).
Axes of the slice: x: 2, y: 2, z: 4, core: 2. Of those that a mesh axis runs over, the one named last changes fastest.
Arguments:
- features: bfloat16 [1024, 4, 7680], P('replica', None, 'tensor'), may hold values from -6 to 6
- kv_weight: bfloat16 [7680, 8, 256], P('tensor'), may hold values from -0.0625 to 0.0625
- image_owner: int32 [1024], replicated, may hold values from 0 to 15, as said below
- image_request: int32 [1024], replicated, may hold values from 0 to 7, as said below
- cross_query: bfloat16 [128, 64, 128], P('replica', 'tensor'), may hold values from -6 to 6
- self_query: bfloat16 [128, 64, 128], P('replica', 'tensor'), may hold values from -2.5 to 2.5
- self_cache: bfloat16 [128, 128, 8, 256], P('replica', None, 'tensor'), may hold values from -2.5 to 2.5
- fresh_key_value: bfloat16 [128, 8, 256], P('replica', 'tensor'), may hold values from -2.5 to 2.5
- cache_len: int32 [128], P('replica'), may hold values from 1 to 128, 8192 in all
Outputs:
- cross_out: bfloat16 [128, 64, 128], P('replica', 'tensor')
- self_out: bfloat16 [128, 64, 128], P('replica', 'tensor')
The draws below stay inside these ranges and needn't reach their ends.
Inputs may be any that keep to these rules, and one draw needn't show every extreme that they name: `image_owner`: within each aligned block of 64 consecutive images (the images of one replica group), no decode replica owns more than 8 images, and one decode replica owns exactly 8 images in every block. `image_request`: some requests have no image.
All inputs are finite; a program needn't handle non-finite values. No bound on the sum of `cache_len` on one device may be relied on, other than what follows from the above.
Results may differ from the reference program's by a relative error of at most 0.02.
Values may be sent and summed in bfloat16 or wider, within the bound.
A program may use at most 128 MiB of HBM per device.

```python
import math
import jax
import jax.numpy as jnp
import numpy as np
from jax import lax

VW = 7680
HEADS = 64
KVH = 8
HEAD_SIZE = 128
IMG_ENC = 64
PATCHES = 4
REQ = 8
CACHE = 128
CAP = 8
IMAGE_TOTAL = 1024
REQS = 128
N_REPLICA = 16
N_TENSOR = 2


def owner_table(key):
    key_hot, key_blocks = jax.random.split(jax.random.fold_in(key, 71))
    hot = jax.random.randint(key_hot, (), 0, N_REPLICA).astype(jnp.int32)

    def one_block(block_key):
        key_perm, key_shuffle = jax.random.split(block_key)
        perm = jax.random.permutation(key_perm, N_REPLICA * CAP).astype(jnp.int32)
        dests = perm % N_REPLICA
        is_hot = (dests == hot).astype(jnp.int32)
        order = jnp.argsort(is_hot, stable=True)
        others = dests[order][:IMG_ENC - CAP]
        chosen = jnp.concatenate([jnp.full((CAP,), hot, jnp.int32), others])
        return chosen[jax.random.permutation(key_shuffle, IMG_ENC)]
    keys = jax.random.split(key_blocks, N_REPLICA)
    return jax.vmap(one_block)(keys).reshape(IMAGE_TOTAL).astype(jnp.int32)


def draw_image_owner(key, part):
    return owner_table(key)


def draw_image_request(key, part):
    owners = owner_table(key)
    key_perm, key_empty, key_some, key_every = jax.random.split(jax.random.fold_in(key, 73), 4)
    perm = jax.random.permutation(key_perm, N_REPLICA).astype(jnp.int32)
    flagged = (perm < N_REPLICA // 2).astype(jnp.int32)
    empty = jax.random.randint(key_empty, (N_REPLICA,), 0, REQ).astype(jnp.int32)
    some = jax.random.randint(key_some, (IMAGE_TOTAL,), 0, REQ - 1).astype(jnp.int32)
    every = jax.random.randint(key_every, (IMAGE_TOTAL,), 0, REQ).astype(jnp.int32)
    empty_image = empty[owners]
    flag_image = flagged[owners]
    skipped = some + (some >= empty_image).astype(jnp.int32)
    return jnp.where(flag_image > 0, skipped, every).astype(jnp.int32)


def level_of(key, dims, cuts, least, largest):
    def one(axis_at, blocks):
        heights = jax.random.uniform(jax.random.fold_in(jax.random.fold_in(key, 6), axis_at), (blocks,), jnp.float32, least / len(cuts), largest / len(cuts))
        return jnp.repeat(jnp.exp(heights), dims[axis_at] // blocks).reshape((-1,) + (1,) * (len(dims) - axis_at - 1))

    level = one(*cuts[0])
    for cut in cuts[1:]:
        level = level * one(*cut)
    return level


def split_up(number_of, total, reach, skew):
    weights = [(1 << 20) // math.isqrt(grade ** skew) + 1 for grade in range(2, number_of + 1)]
    spare, given = total - reach - (number_of - 1), [1] * (number_of - 1)
    while spare > 0:
        free = [i for i in range(number_of - 1) if given[i] < reach]
        pool, budget = sum([weights[i] for i in free]), spare
        for i in free:
            more = min(reach - given[i], max(1, budget * weights[i] // pool), spare)
            given[i] = given[i] + more
            spare = spare - more
    return np.array([reach] + given)


def ragged(stream_key, count, total, bound, slope):
    if count == 2:
        one = jax.random.randint(stream_key, (), max(1, total - bound), min(bound, total - 1) + 1)
        return jnp.stack([one, total - one])
    tallies = jnp.asarray(split_up(count, total, bound, slope), jnp.int32)
    couples = (count - 1) // 2
    donor, taker = tallies[1:1 + 2 * couples:2], tallies[2:2 + 2 * couples:2]
    room = jnp.minimum(donor - 1, bound - taker)
    shifted = jax.random.randint(jax.random.fold_in(stream_key, 1), (couples,), 0, 1 << 20) % (room + 1)
    tallies = tallies.at[1:1 + 2 * couples:2].set(donor - shifted).at[2:2 + 2 * couples:2].set(taker + shifted)
    return tallies[jax.random.permutation(jax.random.fold_in(stream_key, 2), count)]


def noise(key, dims, spread, bound, shards=(), held_as=jnp.bfloat16):
    drawn = spread * jax.random.normal(key, dims, jnp.float32)
    if shards:
        drawn = drawn * level_of(key, dims, shards, -0.22, 0.18)
    return jnp.clip(drawn, -bound, bound).astype(held_as)


def setup_inputs(seed: int = 0) -> dict:
    arg_keys = jax.random.split(jax.random.key(seed), 10)
    return {
        "features": noise(arg_keys[0], (IMAGE_TOTAL, PATCHES, VW), 1.0, 6.0, ((0, 16), (2, 2))),
        "kv_weight": noise(arg_keys[1], (VW, KVH, 2 * HEAD_SIZE), VW ** -0.5, 0.0625, ((0, 2),)),
        "image_owner": draw_image_owner(jax.random.fold_in(arg_keys[9], 71), 0),
        "image_request": draw_image_request(jax.random.fold_in(arg_keys[9], 71), 0),
        "cross_query": noise(arg_keys[4], (REQS, HEADS, HEAD_SIZE), 1.0, 6.0, ((0, 16), (1, 2))),
        "self_query": noise(arg_keys[5], (REQS, HEADS, HEAD_SIZE), 1.0, 2.5, ((0, 16), (1, 2))),
        "self_cache": noise(arg_keys[6], (REQS, CACHE, KVH, 2 * HEAD_SIZE), 1.0, 2.5, ((0, 16), (2, 2))),
        "fresh_key_value": noise(arg_keys[7], (REQS, KVH, 2 * HEAD_SIZE), 1.0, 2.5, ((0, 16), (1, 2))),
        "cache_len": ragged(arg_keys[8], REQS, REQS * CACHE // 2, CACHE, 2).astype(jnp.int32),
    }


def reference(features, kv_weight, image_owner, image_request, cross_query, self_query, self_cache, fresh_key_value, cache_len):
    block = VW // N_TENSOR
    rows = features.reshape(IMAGE_TOTAL * PATCHES, VW)
    weight_flat = kv_weight.reshape(VW, KVH * 2 * HEAD_SIZE)
    score_scale = 1.0 / math.sqrt(HEAD_SIZE)

    def add_block(j, total):
        cols = lax.dynamic_slice_in_dim(rows, j * block, block, 1)
        wrows = lax.dynamic_slice_in_dim(weight_flat, j * block, block, 0)
        part = jnp.dot(cols, wrows, preferred_element_type=jnp.float32).astype(jnp.bfloat16)
        part = lax.optimization_barrier(part)
        return total + part.astype(jnp.float32)
    summed = lax.fori_loop(0, N_TENSOR, add_block, jnp.zeros((IMAGE_TOTAL * PATCHES, KVH * 2 * HEAD_SIZE), jnp.float32))
    image_kv = summed.astype(jnp.bfloat16).reshape(IMAGE_TOTAL, PATCHES, KVH, 2 * HEAD_SIZE)
    unscaled_keys = image_kv[..., :HEAD_SIZE].astype(jnp.float32)
    image_keys = (unscaled_keys * lax.rsqrt(lax.optimization_barrier(jnp.mean(unscaled_keys * unscaled_keys, axis=-1, keepdims=True)) + 1e-05)).astype(jnp.bfloat16)
    image_values = image_kv[..., HEAD_SIZE:]
    order = jnp.argsort(image_owner, stable=True).astype(jnp.int32)
    owner_ids = jnp.arange(N_REPLICA, dtype=jnp.int32)
    counts = lax.optimization_barrier(jnp.sum((image_owner[None, :] == owner_ids[:, None]).astype(jnp.int32), axis=1, dtype=jnp.int32))
    starts = (jnp.cumsum(counts, dtype=jnp.int32) - counts).astype(jnp.int32)
    most = N_REPLICA * CAP
    padded = jnp.concatenate([order, jnp.zeros((most,), jnp.int32)])
    group = HEADS // KVH
    queries = cross_query.reshape(N_REPLICA, REQ, KVH, group, HEAD_SIZE)
    slots = jnp.arange(most, dtype=jnp.int32)
    req_ids = jnp.arange(REQ, dtype=jnp.int32)

    def one_owner(owner):
        idx = lax.dynamic_slice_in_dim(padded, starts[owner], most).astype(jnp.int32)
        valid = slots < counts[owner]
        keys = image_keys[idx].astype(jnp.float32)
        values = image_values[idx].astype(jnp.float32)
        req = image_request[idx]
        mask = valid[None, :] & (req[None, :] == req_ids[:, None])
        query = queries[owner].astype(jnp.float32)
        scores = jnp.einsum('bkgd,ipkd->bkgip', query, keys) * score_scale
        weight = jnp.where(mask[:, None, None, :, None], jnp.exp(scores), jnp.float32(0.0))
        total = lax.optimization_barrier(jnp.sum(weight, axis=(3, 4)))
        rounded = lax.optimization_barrier(weight.astype(jnp.bfloat16))
        numer = jnp.einsum('bkgip,ipkd->bkgd', rounded.astype(jnp.float32), values)
        has_image = jnp.any(mask, axis=1)
        safe = jnp.where(has_image[:, None, None], total, jnp.float32(1.0))
        result = jnp.where(has_image[:, None, None, None], numer / safe[..., None], jnp.float32(0.0))
        return result.astype(jnp.bfloat16)
    cross_out = lax.map(one_owner, owner_ids).reshape(REQS, HEADS, HEAD_SIZE)
    self_query_rows = self_query.reshape(REQS, KVH, group, HEAD_SIZE).astype(jnp.float32)
    cache_keys = self_cache[..., :HEAD_SIZE].astype(jnp.float32)
    cache_values = self_cache[..., HEAD_SIZE:].astype(jnp.float32)
    scores = jnp.einsum('bkgd,bskd->bkgs', self_query_rows, cache_keys) * score_scale
    live = jnp.arange(CACHE, dtype=jnp.int32)[None, :] < cache_len[:, None]
    weight = jnp.where(live[:, None, None, :], jnp.exp(scores), jnp.float32(0.0))
    fresh_weight = jnp.exp(jnp.einsum('ptwe,pte->ptw', self_query_rows, fresh_key_value[..., :HEAD_SIZE].astype(jnp.float32)) * score_scale)
    total = lax.optimization_barrier(jnp.sum(weight, axis=-1)) + fresh_weight
    rounded = lax.optimization_barrier(weight.astype(jnp.bfloat16))
    new_rounded = lax.optimization_barrier(fresh_weight.astype(jnp.bfloat16))
    numer = jnp.einsum('bkgs,bskd->bkgd', rounded.astype(jnp.float32), cache_values)
    numer = numer + new_rounded.astype(jnp.float32)[..., None] * fresh_key_value[:, :, None, HEAD_SIZE:].astype(jnp.float32)
    self_out = (numer / total[..., None]).astype(jnp.bfloat16).reshape(REQS, HEADS, HEAD_SIZE)
    return (cross_out, self_out)
```

```python
import functools
import math

import jax
import jax.numpy as jnp
from jax import lax
from jax.experimental import pallas as pl
from jax.experimental.pallas import tpu as pltpu
from jax.sharding import PartitionSpec as P

MESH = pl.DeviceIdType.MESH
F32 = jnp.float32
BF16 = jnp.bfloat16


def project_kernel(kvh, group_rows, perm_ref, feat_ref, w_ref, out_ref, by_head, acc):
    step = pl.program_id(0)
    chunk = feat_ref.shape[1]
    width = w_ref.shape[1]
    tile = kvh * group_rows

    @pl.when(step == 0)
    def _():
        acc[...] = jnp.zeros_like(acc)

    perm = perm_ref[...]
    for g in range(chunk // group_rows):
        moved = jnp.dot(
            perm, w_ref[g * tile : (g + 1) * tile, :], preferred_element_type=F32
        ).astype(BF16)
        for h in range(kvh):
            by_head[h, g * group_rows : (g + 1) * group_rows, :] = moved[
                h * group_rows : (h + 1) * group_rows, :
            ]
    feat = feat_ref[...]
    for h in range(kvh):
        acc[:, h * width : (h + 1) * width] += jnp.dot(
            feat, by_head[h], preferred_element_type=F32
        )

    @pl.when(step == pl.num_programs(0) - 1)
    def _():
        n_ten, _, cols = out_ref.shape
        for t in range(n_ten):
            out_ref[t] = acc[:, t * cols : (t + 1) * cols].astype(BF16)


def project(feat, weight, n_ten):
    rows, depth = feat.shape
    kvh, width = weight.shape[1:]
    group_rows = 256 // kvh
    tile = kvh * group_rows
    chunk = depth
    for c in range(128, 385, 128):
        if depth % c == 0:
            chunk = c
    at = jnp.arange(tile, dtype=jnp.int32)
    source = (at % group_rows) * kvh + at // group_rows
    perm = (source[:, None] == at[None, :]).astype(BF16)
    cols = kvh * width // n_ten
    return pl.pallas_call(
        functools.partial(project_kernel, kvh, group_rows),
        grid=(depth // chunk,),
        in_specs=[
            pl.BlockSpec((tile, tile), lambda k: (0, 0)),
            pl.BlockSpec((rows, chunk), lambda k: (0, k)),
            pl.BlockSpec((chunk * kvh, width), lambda k: (k, 0)),
        ],
        out_specs=pl.BlockSpec((n_ten, rows, cols), lambda k: (0, 0, 0)),
        out_shape=jax.ShapeDtypeStruct((n_ten, rows, cols), BF16),
        scratch_shapes=[
            pltpu.VMEM((kvh, chunk, width), BF16),
            pltpu.VMEM((rows, kvh * width), F32),
        ],
        compiler_params=pltpu.CompilerParams(vmem_limit_bytes=40 * 1024 * 1024),
        cost_estimate=pl.CostEstimate(
            flops=4 * rows * depth * kvh * width,
            bytes_accessed=2 * depth * (kvh * width + rows),
            transcendentals=0,
        ),
    )(perm, feat, weight.reshape(depth * kvh, width))


def attend_kernel(
    n_rep,
    n_ten,
    kvh,
    len_ref,
    part_ref,
    slot_ref,
    code_ref,
    cq_ref,
    sq_ref,
    cache_ref,
    fresh_ref,
    cross_ref,
    self_ref,
    got_t,
    outgoing,
    arrived,
    send_t,
    recv_t,
    send_r,
    recv_r,
):
    rep = lax.axis_index("replica")
    ten = lax.axis_index("tensor")
    reqs, heads, width = cq_ref.shape
    group = heads // kvh
    scale = 1.0 / math.sqrt(width)
    slot_rows = outgoing.shape[1]

    barrier = pltpu.get_barrier_semaphore()
    for d in range(1, n_ten):
        peer = lax.rem(ten + d, n_ten)
        pl.semaphore_signal(barrier, inc=1, device_id=(rep, peer), device_id_type=MESH)
    for d in range(1, n_rep):
        peer = lax.rem(rep + d, n_rep)
        pl.semaphore_signal(barrier, inc=1, device_id=(peer, ten), device_id_type=MESH)
    pl.semaphore_wait(barrier, n_ten + n_rep - 2)

    to_ten = []
    for d in range(1, n_ten):
        peer = lax.rem(ten + d, n_ten)
        copy = pltpu.make_async_remote_copy(
            src_ref=part_ref.at[peer],
            dst_ref=got_t.at[d - 1],
            send_sem=send_t.at[d - 1],
            recv_sem=recv_t.at[d - 1],
            device_id=(rep, peer),
            device_id_type=MESH,
        )
        copy.start()
        to_ten.append(copy)
    rows = part_ref.shape[1]
    at = lax.broadcasted_iota(jnp.int32, (n_rep * slot_rows, rows), 0)
    placing = (at == slot_ref[...]).astype(BF16)
    kv = part_ref[ten].astype(F32)
    for d in range(1, n_ten):
        to_ten[d - 1].wait_recv()
        kv = kv + got_t[d - 1].astype(F32)
    kv = kv.astype(BF16)
    placed = jnp.dot(placing, kv, preferred_element_type=F32)
    outgoing[...] = placed.reshape(outgoing.shape).astype(BF16)
    to_rep = []
    for d in range(1, n_rep):
        peer = lax.rem(rep + d, n_rep)
        copy = pltpu.make_async_remote_copy(
            src_ref=outgoing.at[peer],
            dst_ref=arrived.at[d],
            send_sem=send_r.at[d],
            recv_sem=recv_r.at[d],
            device_id=(peer, ten),
            device_id_type=MESH,
        )
        copy.start()
        to_rep.append(copy)
    arrived[0] = outgoing[rep]

    places = cache_ref.shape[1]
    col = lax.broadcasted_iota(jnp.int32, (heads, places), 1)
    row = lax.broadcasted_iota(jnp.int32, (heads, places), 0)
    same_head = lax.rem(col, kvh) == row // group
    for b in range(reqs):
        query = sq_ref[b]
        keys = cache_ref[b, :, :width]
        values = cache_ref[b, :, width:]
        score = (
            lax.dot_general(query, keys, (((1,), (1,)), ((), ())), preferred_element_type=F32)
            * scale
        )
        live = same_head & (col // kvh < len_ref[b])
        weight = jnp.where(live, jnp.exp(score), 0.0)
        fresh = fresh_ref[b].astype(F32)
        fresh_weight = jnp.exp(
            jnp.sum(query.astype(F32) * fresh[:, :width], axis=1, keepdims=True) * scale
        )
        total = jnp.sum(weight, axis=1, keepdims=True) + fresh_weight
        numer = jnp.dot(weight.astype(BF16), values, preferred_element_type=F32)
        numer = numer + fresh_weight.astype(BF16).astype(F32) * fresh[:, width:]
        self_ref[b] = (numer / total).astype(BF16)

    cross_query = cq_ref[...].astype(F32)
    queries = [
        cross_query[:, h * group : (h + 1) * group, :].reshape(reqs * group, width).astype(BF16)
        for h in range(kvh)
    ]
    total = [jnp.zeros((reqs * group, 1), F32)] * kvh
    numer = [jnp.zeros((reqs * group, width), F32)] * kvh
    batch = max(1, 128 // slot_rows)
    batch = min(batch, n_rep)
    count = jnp.zeros((reqs * group, 1), F32)
    for first in range(0, n_rep, batch):
        for d in range(max(1, first), first + batch):
            to_rep[d - 1].wait_recv()
        size = batch * slot_rows
        code = code_ref[:, first * slot_rows : first * slot_rows + size]
        owner_row = lax.broadcasted_iota(jnp.int32, (reqs * group, size), 0) // group
        mask = owner_row == code
        count = count + jnp.sum(mask.astype(F32), axis=1, keepdims=True)
        for h in range(kvh):
            both = arrived[first : first + batch, :, h * 2 * width : (h + 1) * 2 * width]
            both = both.astype(F32).reshape(size, 2 * width)
            raw = both[:, :width]
            keys = (
                raw * lax.rsqrt(jnp.mean(raw * raw, axis=1, keepdims=True) + 1e-05)
            ).astype(BF16)
            values = both[:, width:].astype(BF16)
            score = (
                lax.dot_general(
                    queries[h], keys, (((1,), (1,)), ((), ())), preferred_element_type=F32
                )
                * scale
            )
            weight = jnp.where(mask, jnp.exp(score), 0.0)
            total[h] = total[h] + jnp.sum(weight, axis=1, keepdims=True)
            numer[h] = numer[h] + jnp.dot(
                weight.astype(BF16), values, preferred_element_type=F32
            )
    has = count > 0.0
    parts = []
    for h in range(kvh):
        safe = jnp.where(has, total[h], 1.0)
        parts.append(jnp.where(has, numer[h] / safe, 0.0).reshape(reqs, group, width))
    cross_ref[...] = jnp.concatenate(parts, axis=1).astype(BF16)

    for copy in to_ten:
        copy.wait_send()
    for copy in to_rep:
        copy.wait_send()


def local(
    n_rep,
    n_ten,
    features,
    kv_weight,
    image_owner,
    image_request,
    cross_query,
    self_query,
    self_cache,
    fresh_key_value,
    cache_len,
):
    me = lax.axis_index("replica")
    images, patches, depth = features.shape
    reqs, heads, width = cross_query.shape
    kvh = self_cache.shape[2]
    group = heads // kvh
    slot_cap = max(2, 2 * images // n_rep)
    rows = images * patches
    slot_rows = slot_cap * patches

    owners = image_owner.reshape(n_rep, images)
    requests = image_request.reshape(n_rep, images)
    mine = lax.dynamic_index_in_dim(owners, me, 0, keepdims=False)
    at = jnp.arange(images, dtype=jnp.int32)
    earlier = (mine[:, None] == mine[None, :]) & (at[:, None] > at[None, :])
    rank = jnp.sum(earlier.astype(jnp.int32), axis=1, dtype=jnp.int32)
    slot = mine * slot_cap + rank
    slot_row = (slot[:, None] * patches + jnp.arange(patches, dtype=jnp.int32)[None, :]).reshape(
        1, rows
    )

    source = lax.rem(me - jnp.arange(n_rep, dtype=jnp.int32) + n_rep, n_rep)
    from_owner = owners[source]
    match = from_owner == me
    before = (at[:, None] < at[None, :]).astype(BF16)
    place = jnp.dot(match.astype(BF16), before, preferred_element_type=F32).astype(jnp.int32)
    chosen = match[:, None, :] & (
        place[:, None, :] == jnp.arange(slot_cap, dtype=jnp.int32)[None, :, None]
    )
    code = jnp.sum(jnp.where(chosen, requests[source][:, None, :] + 1, 0), axis=-1) - 1
    code = jnp.broadcast_to(code[:, :, None], (n_rep, slot_cap, patches)).reshape(
        1, n_rep * slot_rows
    )

    part = project(features.reshape(rows, depth), kv_weight, n_ten)
    cache = self_cache.reshape(reqs, self_cache.shape[1] * kvh, 2 * width)
    fresh = jnp.broadcast_to(
        fresh_key_value[:, :, None, :], (reqs, kvh, group, 2 * width)
    ).reshape(reqs, heads, 2 * width)
    cols = kvh * 2 * width
    vmem = pl.BlockSpec(memory_space=pltpu.VMEM)
    return pl.pallas_call(
        functools.partial(attend_kernel, n_rep, n_ten, kvh),
        in_specs=[pl.BlockSpec(memory_space=pltpu.SMEM)] + [vmem] * 7,
        out_specs=(vmem, vmem),
        out_shape=(
            jax.ShapeDtypeStruct(cross_query.shape, BF16),
            jax.ShapeDtypeStruct(self_query.shape, BF16),
        ),
        scratch_shapes=[
            pltpu.VMEM((n_ten - 1, rows, cols), BF16),
            pltpu.VMEM((n_rep, slot_rows, cols), BF16),
            pltpu.VMEM((n_rep, slot_rows, cols), BF16),
            pltpu.SemaphoreType.DMA((n_ten - 1,)),
            pltpu.SemaphoreType.DMA((n_ten - 1,)),
            pltpu.SemaphoreType.DMA((n_rep,)),
            pltpu.SemaphoreType.DMA((n_rep,)),
        ],
        compiler_params=pltpu.CompilerParams(
            collective_id=0,
            has_side_effects=True,
            vmem_limit_bytes=40 * 1024 * 1024,
        ),
    )(cache_len, part, slot_row, code, cross_query, self_query, cache, fresh)


def solution(mesh):
    n_rep, n_ten = mesh.shape["replica"], mesh.shape["tensor"]
    return jax.shard_map(
        functools.partial(local, n_rep, n_ten),
        mesh=mesh,
        in_specs=(
            P("replica", None, "tensor"),
            P("tensor", None, None),
            P(),
            P(),
            P("replica", "tensor", None),
            P("replica", "tensor", None),
            P("replica", None, "tensor", None),
            P("replica", "tensor", None),
            P("replica"),
        ),
        out_specs=(P("replica", "tensor", None), P("replica", "tensor", None)),
        check_vma=False,
    )
```

```python
import functools
import math

import jax
import jax.numpy as jnp
from jax import lax
from jax.experimental import pallas as pl
from jax.experimental.pallas import tpu as pltpu
from jax.sharding import PartitionSpec as P

MESH = pl.DeviceIdType.MESH
F32 = jnp.float32
BF16 = jnp.bfloat16


def step_kernel(
    n_rep,
    n_ten,
    kvh_all,
    kvh,
    len_ref,
    slot_ref,
    code_ref,
    perm_ref,
    feat_ref,
    w_ref,
    cq_ref,
    sq_ref,
    cache_hbm,
    fresh_ref,
    cross_ref,
    self_ref,
    feat,
    by_head,
    acc,
    part,
    got,
    outgoing,
    arrived,
    weights,
    cache_ref,
    cache_sem,
    send_t,
    recv_t,
    send_r,
    recv_r,
):
    rep = lax.axis_index("replica")
    ten = lax.axis_index("tensor")
    half = pl.program_id(0)
    step = pl.program_id(1)
    steps = pl.num_programs(1)
    reqs, heads, width = cq_ref.shape
    group = heads // kvh
    scale = 1.0 / math.sqrt(width)
    slot_rows = outgoing.shape[2]
    cols = kvh * width
    rows, chunk = feat.shape[1:]
    run = 256 // kvh_all
    tile = run * kvh_all
    cache_copy = pltpu.make_async_copy(cache_hbm, cache_ref, cache_sem)

    def to_ten(which, d):
        peer = lax.rem(ten + d, n_ten)
        return pltpu.make_async_remote_copy(
            src_ref=part.at[which, peer],
            dst_ref=got.at[which, d - 1],
            send_sem=send_t.at[which, d - 1],
            recv_sem=recv_t.at[which, d - 1],
            device_id=(rep, peer),
            device_id_type=MESH,
        )

    def to_rep(which, d):
        peer = lax.rem(rep + d, n_rep)
        return pltpu.make_async_remote_copy(
            src_ref=outgoing.at[which, peer],
            dst_ref=arrived.at[which, d],
            send_sem=send_r.at[which, d],
            recv_sem=recv_r.at[which, d],
            device_id=(peer, ten),
            device_id_type=MESH,
        )

    def route(which):
        at = lax.broadcasted_iota(jnp.int32, (n_rep * slot_rows, rows), 0)
        placing = (at == slot_ref[...]).astype(BF16)
        kv = part[which, ten].astype(F32)
        for d in range(1, n_ten):
            to_ten(which, d).wait_recv()
            kv = kv + got[which, d - 1].astype(F32)
        placed = jnp.dot(placing, kv.astype(BF16), preferred_element_type=F32)
        outgoing[which] = placed.reshape(n_rep, slot_rows, cols).astype(BF16)
        for d in range(1, n_rep):
            to_rep(which, d).start()
        arrived[which, 0] = outgoing[which, rep]

    @pl.when((half == 0) & (step == 0))
    def _():
        barrier = pltpu.get_barrier_semaphore()
        for d in range(1, n_ten):
            peer = lax.rem(ten + d, n_ten)
            pl.semaphore_signal(barrier, inc=1, device_id=(rep, peer), device_id_type=MESH)
        for d in range(1, n_rep):
            peer = lax.rem(rep + d, n_rep)
            pl.semaphore_signal(barrier, inc=1, device_id=(peer, ten), device_id_type=MESH)
        cache_copy.start()

    @pl.when(half == 0)
    def _():
        feat[step] = feat_ref[...].astype(F32).reshape(rows, chunk).astype(BF16)

    @pl.when(step == 0)
    def _():
        acc[...] = jnp.zeros_like(acc)

    perm = perm_ref[...]
    for g in range(0, chunk // run, 2):
        two = jnp.concatenate(
            [w_ref[g * tile : (g + 1) * tile, :], w_ref[(g + 1) * tile : (g + 2) * tile, :]],
            axis=1,
        )
        moved = jnp.dot(perm, two, preferred_element_type=F32).astype(BF16)
        for h in range(kvh_all):
            lanes = (h % 2) * width
            for q in range(2):
                by_head[
                    h // 2, (g + q) * run : (g + q + 1) * run, lanes : lanes + width
                ] = moved[h * run : (h + 1) * run, q * width : (q + 1) * width]
    now = feat[step]
    for p in range(kvh_all // 2):
        acc[:, p * 2 * width : (p + 1) * 2 * width] += jnp.dot(
            now, by_head[p], preferred_element_type=F32
        )

    @pl.when(step == steps - 1)
    def _():
        for t in range(n_ten):
            part[half, t] = acc[:, t * cols : (t + 1) * cols].astype(BF16)

    @pl.when((half == 0) & (step == steps - 1))
    def _():
        pl.semaphore_wait(pltpu.get_barrier_semaphore(), n_ten + n_rep - 2)
        for d in range(1, n_ten):
            to_ten(0, d).start()

    @pl.when((half == 1) & (step == jnp.minimum(1, steps - 1)))
    def _():
        route(0)

    @pl.when((half == 1) & (step == steps - 1))
    def _():
        for d in range(1, n_ten):
            to_ten(1, d).start()
        route(1)

        cache_copy.wait()
        places = cache_ref.shape[1] * kvh
        col = lax.broadcasted_iota(jnp.int32, (heads, places), 1)
        row = lax.broadcasted_iota(jnp.int32, (heads, places), 0)
        same_head = lax.rem(col, kvh) == row // group
        for b in range(reqs):
            query = sq_ref[b]
            both = cache_ref[b].astype(F32).reshape(places, 2 * width).astype(BF16)
            score = (
                lax.dot_general(
                    query, both[:, :width], (((1,), (1,)), ((), ())), preferred_element_type=F32
                )
                * scale
            )
            live = same_head & (col // kvh < len_ref[b])
            weight = jnp.where(live, jnp.exp(score), 0.0)
            fresh = fresh_ref[b].astype(F32)
            fresh_weight = jnp.exp(
                jnp.sum(query.astype(F32) * fresh[:, :width], axis=1, keepdims=True) * scale
            )
            total = jnp.sum(weight, axis=1, keepdims=True) + fresh_weight
            numer = jnp.dot(
                weight.astype(BF16), both[:, width:], preferred_element_type=F32
            )
            numer = numer + fresh_weight.astype(BF16).astype(F32) * fresh[:, width:]
            self_ref[b] = (numer / total).astype(BF16)

        cross_query = cq_ref[...].astype(F32)
        size = n_rep * slot_rows
        owner_row = lax.broadcasted_iota(jnp.int32, (reqs * group, size), 0) // group
        mask = owner_row == code_ref[...]
        has = jnp.sum(mask.astype(F32), axis=1, keepdims=True) > 0.0
        for d in range(1, n_rep):
            to_rep(0, d).wait_recv()
        safe = []
        for h in range(kvh):
            query = cross_query[:, h * group : (h + 1) * group, :]
            query = query.reshape(reqs * group, width).astype(BF16)
            raw = arrived[0, :, :, h * width : (h + 1) * width].astype(F32).reshape(size, width)
            keys = (
                raw * lax.rsqrt(jnp.mean(raw * raw, axis=1, keepdims=True) + 1e-05)
            ).astype(BF16)
            score = (
                lax.dot_general(
                    query, keys, (((1,), (1,)), ((), ())), preferred_element_type=F32
                )
                * scale
            )
            weight = jnp.where(mask, jnp.exp(score), 0.0)
            safe.append(jnp.where(has, jnp.sum(weight, axis=1, keepdims=True), 1.0))
            weights[h] = weight.astype(BF16)
        for d in range(1, n_rep):
            to_rep(1, d).wait_recv()
        parts = []
        for h in range(kvh):
            values = arrived[1, :, :, h * width : (h + 1) * width]
            values = values.astype(F32).reshape(size, width).astype(BF16)
            numer = jnp.dot(weights[h], values, preferred_element_type=F32)
            parts.append(jnp.where(has, numer / safe[h], 0.0).reshape(reqs, group, width))
        cross_ref[...] = jnp.concatenate(parts, axis=1).astype(BF16)

        for which in range(2):
            for d in range(1, n_ten):
                to_ten(which, d).wait_send()
            for d in range(1, n_rep):
                to_rep(which, d).wait_send()


def local(
    n_rep,
    n_ten,
    features,
    kv_weight,
    image_owner,
    image_request,
    cross_query,
    self_query,
    self_cache,
    fresh_key_value,
    cache_len,
):
    me = lax.axis_index("replica")
    images, patches, depth = features.shape
    reqs, heads, width = cross_query.shape
    kvh = self_cache.shape[2]
    kvh_all = kv_weight.shape[1]
    group = heads // kvh
    slot_cap = max(2, 2 * images // n_rep)
    rows = images * patches
    slot_rows = slot_cap * patches

    ids = (image_owner * reqs + image_request).reshape(n_rep, images)
    owners = ids // reqs
    mine = lax.dynamic_index_in_dim(ids, me, 0, keepdims=False) // reqs
    at = jnp.arange(images, dtype=jnp.int32)
    earlier = (mine[:, None] == mine[None, :]) & (at[:, None] > at[None, :])
    rank = jnp.sum(earlier.astype(jnp.int32), axis=1, dtype=jnp.int32)
    slot = mine * slot_cap + rank
    slot_row = (slot[:, None] * patches + jnp.arange(patches, dtype=jnp.int32)[None, :]).reshape(
        1, rows
    )

    match = owners == me
    before = (at[:, None] < at[None, :]).astype(BF16)
    place = jnp.dot(match.astype(BF16), before, preferred_element_type=F32).astype(jnp.int32)
    chosen = match[:, None, :] & (
        place[:, None, :] == jnp.arange(slot_cap, dtype=jnp.int32)[None, :, None]
    )
    code = jnp.sum(jnp.where(chosen, (ids - me * reqs)[:, None, :] + 1, 0), axis=-1) - 1
    source = lax.rem(me - jnp.arange(n_rep, dtype=jnp.int32) + n_rep, n_rep)
    turn = source[:, None] == jnp.arange(n_rep, dtype=jnp.int32)[None, :]
    code = jnp.sum(jnp.where(turn[:, :, None], code[None], 0), axis=1)
    code = jnp.broadcast_to(code[:, :, None], (n_rep, slot_cap, patches)).reshape(
        1, n_rep * slot_rows
    )

    tile = 256 // kvh_all * kvh_all
    spot = jnp.arange(tile, dtype=jnp.int32)
    origin = (spot % (tile // kvh_all)) * kvh_all + spot // (tile // kvh_all)
    perm = (origin[:, None] == spot[None, :]).astype(BF16)
    fresh = jnp.broadcast_to(
        fresh_key_value[:, :, None, :], (reqs, kvh, group, 2 * width)
    ).reshape(reqs, heads, 2 * width)
    chunk = depth
    for c in range(128, 385, 128):
        if depth % c == 0:
            chunk = c
    steps = depth // chunk
    cols = kvh * width
    vmem = pl.BlockSpec(memory_space=pltpu.VMEM)
    return pl.pallas_call(
        functools.partial(step_kernel, n_rep, n_ten, kvh_all, kvh),
        grid=(2, steps),
        in_specs=[
            pl.BlockSpec(memory_space=pltpu.SMEM),
            vmem,
            vmem,
            vmem,
            pl.BlockSpec(
                (images, patches, chunk), lambda j, k: (0, 0, k * (1 - j) + (steps - 1) * j)
            ),
            pl.BlockSpec((chunk * kvh_all, width), lambda j, k: (k, j)),
            vmem,
            vmem,
            pl.BlockSpec(memory_space=pl.ANY),
            vmem,
        ],
        out_specs=(vmem, vmem),
        out_shape=(
            jax.ShapeDtypeStruct(cross_query.shape, BF16),
            jax.ShapeDtypeStruct(self_query.shape, BF16),
        ),
        scratch_shapes=[
            pltpu.VMEM((steps, rows, chunk), BF16),
            pltpu.VMEM((kvh_all // 2, chunk, 2 * width), BF16),
            pltpu.VMEM((rows, kvh_all * width), F32),
            pltpu.VMEM((2, n_ten, rows, cols), BF16),
            pltpu.VMEM((2, n_ten - 1, rows, cols), BF16),
            pltpu.VMEM((2, n_rep, slot_rows, cols), BF16),
            pltpu.VMEM((2, n_rep, slot_rows, cols), BF16),
            pltpu.VMEM((kvh, reqs * group, n_rep * slot_rows), BF16),
            pltpu.VMEM(self_cache.shape, BF16),
            pltpu.SemaphoreType.DMA,
            pltpu.SemaphoreType.DMA((2, n_ten - 1)),
            pltpu.SemaphoreType.DMA((2, n_ten - 1)),
            pltpu.SemaphoreType.DMA((2, n_rep)),
            pltpu.SemaphoreType.DMA((2, n_rep)),
        ],
        compiler_params=pltpu.CompilerParams(
            collective_id=0,
            has_side_effects=True,
            vmem_limit_bytes=48 * 1024 * 1024,
        ),
    )(
        cache_len,
        slot_row,
        code,
        perm,
        features,
        kv_weight.reshape(depth * kvh_all, 2 * width),
        cross_query,
        self_query,
        self_cache,
        fresh,
    )


def solution(mesh):
    n_rep, n_ten = mesh.shape["replica"], mesh.shape["tensor"]
    return jax.shard_map(
        functools.partial(local, n_rep, n_ten),
        mesh=mesh,
        in_specs=(
            P("replica", None, "tensor"),
            P("tensor", None, None),
            P(),
            P(),
            P("replica", "tensor", None),
            P("replica", "tensor", None),
            P("replica", None, "tensor", None),
            P("replica", "tensor", None),
            P("replica"),
        ),
        out_specs=(P("replica", "tensor", None), P("replica", "tensor", None)),
        check_vma=False,
    )
```

```python
import functools
import math

import jax
import jax.numpy as jnp
from jax import lax
from jax.experimental import pallas as pl
from jax.experimental.pallas import tpu as pltpu
from jax.sharding import PartitionSpec as P

MESH = pl.DeviceIdType.MESH
F32 = jnp.float32
BF16 = jnp.bfloat16


def step_kernel(
    n_rep,
    n_ten,
    kvh_all,
    kvh,
    len_ref,
    slot_ref,
    code_ref,
    perm_ref,
    feat_ref,
    w_ref,
    cq_ref,
    sq_ref,
    cache_hbm,
    fresh_ref,
    cross_ref,
    self_ref,
    feat,
    by_head,
    acc,
    part,
    got,
    outgoing,
    arrived,
    weights,
    cache_ref,
    cache_sem,
    send_t,
    recv_t,
    send_r,
    recv_r,
):
    rep = lax.axis_index("replica")
    ten = lax.axis_index("tensor")
    half = pl.program_id(0)
    step = pl.program_id(1)
    steps = pl.num_programs(1)
    reqs, heads, width = cq_ref.shape
    group = heads // kvh
    scale = 1.0 / math.sqrt(width)
    slot_rows = outgoing.shape[2]
    cols = kvh * width
    rows, chunk = feat.shape[1:]
    run = 256 // kvh_all
    tile = run * kvh_all
    cache_copy = pltpu.make_async_copy(cache_hbm, cache_ref, cache_sem)

    def to_ten(which, d):
        peer = lax.rem(ten + d, n_ten)
        return pltpu.make_async_remote_copy(
            src_ref=part.at[which, peer],
            dst_ref=got.at[which, d - 1],
            send_sem=send_t.at[which, d - 1],
            recv_sem=recv_t.at[which, d - 1],
            device_id=(rep, peer),
            device_id_type=MESH,
        )

    def to_rep(which, d):
        peer = lax.rem(rep + d, n_rep)
        return pltpu.make_async_remote_copy(
            src_ref=outgoing.at[which, peer],
            dst_ref=arrived.at[which, rep],
            send_sem=send_r.at[which, d],
            recv_sem=recv_r.at[which, rep],
            device_id=(peer, ten),
            device_id_type=MESH,
        )

    def wait_arrival(which, d):
        source = lax.rem(rep - d + n_rep, n_rep)
        pltpu.make_async_remote_copy(
            src_ref=outgoing.at[which, source],
            dst_ref=arrived.at[which, source],
            send_sem=send_r.at[which, d],
            recv_sem=recv_r.at[which, source],
            device_id=(source, ten),
            device_id_type=MESH,
        ).wait_recv()

    def route(which):
        at = lax.broadcasted_iota(jnp.int32, (n_rep * slot_rows, rows), 0)
        placing = (at == slot_ref[...]).astype(BF16)
        kv = part[which, ten].astype(F32)
        for d in range(1, n_ten):
            to_ten(which, d).wait_recv()
            kv = kv + got[which, d - 1].astype(F32)
        placed = jnp.dot(placing, kv.astype(BF16), preferred_element_type=F32)
        outgoing[which] = placed.reshape(n_rep, slot_rows, cols).astype(BF16)
        for d in range(1, n_rep):
            to_rep(which, d).start()
        arrived[which, rep] = outgoing[which, rep]

    @pl.when((half == 0) & (step == 0))
    def _():
        barrier = pltpu.get_barrier_semaphore()
        for d in range(1, n_ten):
            peer = lax.rem(ten + d, n_ten)
            pl.semaphore_signal(barrier, inc=1, device_id=(rep, peer), device_id_type=MESH)
        for d in range(1, n_rep):
            peer = lax.rem(rep + d, n_rep)
            pl.semaphore_signal(barrier, inc=1, device_id=(peer, ten), device_id_type=MESH)
        cache_copy.start()

    @pl.when(half == 0)
    def _():
        feat[step] = feat_ref[...].astype(F32).reshape(rows, chunk).astype(BF16)

    @pl.when(step == 0)
    def _():
        acc[...] = jnp.zeros_like(acc)

    perm = perm_ref[...]
    for g in range(0, chunk // run, 2):
        two = jnp.concatenate(
            [w_ref[g * tile : (g + 1) * tile, :], w_ref[(g + 1) * tile : (g + 2) * tile, :]],
            axis=1,
        )
        moved = jnp.dot(perm, two, preferred_element_type=F32).astype(BF16)
        for h in range(kvh_all):
            lanes = (h % 2) * width
            for q in range(2):
                by_head[
                    h // 2, (g + q) * run : (g + q + 1) * run, lanes : lanes + width
                ] = moved[h * run : (h + 1) * run, q * width : (q + 1) * width]
    now = feat[step]
    for p in range(kvh_all // 2):
        acc[:, p * 2 * width : (p + 1) * 2 * width] += jnp.dot(
            now, by_head[p], preferred_element_type=F32
        )

    @pl.when(step == steps - 1)
    def _():
        for t in range(n_ten):
            part[half, t] = acc[:, t * cols : (t + 1) * cols].astype(BF16)

    @pl.when((half == 0) & (step == steps - 1))
    def _():
        pl.semaphore_wait(pltpu.get_barrier_semaphore(), n_ten + n_rep - 2)
        for d in range(1, n_ten):
            to_ten(0, d).start()

    @pl.when((half == 1) & (step == jnp.minimum(1, steps - 1)))
    def _():
        route(0)

    @pl.when((half == 1) & (step == steps - 1))
    def _():
        for d in range(1, n_ten):
            to_ten(1, d).start()
        route(1)

        cache_copy.wait()
        places = cache_ref.shape[1] * kvh
        col = lax.broadcasted_iota(jnp.int32, (heads, places), 1)
        row = lax.broadcasted_iota(jnp.int32, (heads, places), 0)
        same_head = lax.rem(col, kvh) == row // group
        for b in range(reqs):
            query = sq_ref[b]
            both = cache_ref[b].astype(F32).reshape(places, 2 * width).astype(BF16)
            score = (
                lax.dot_general(
                    query, both[:, :width], (((1,), (1,)), ((), ())), preferred_element_type=F32
                )
                * scale
            )
            live = same_head & (col // kvh < len_ref[b])
            weight = jnp.where(live, jnp.exp(score), 0.0)
            fresh = fresh_ref[b].astype(F32)
            fresh_weight = jnp.exp(
                jnp.sum(query.astype(F32) * fresh[:, :width], axis=1, keepdims=True) * scale
            )
            total = jnp.sum(weight, axis=1, keepdims=True) + fresh_weight
            numer = jnp.dot(
                weight.astype(BF16), both[:, width:], preferred_element_type=F32
            )
            numer = numer + fresh_weight.astype(BF16).astype(F32) * fresh[:, width:]
            self_ref[b] = (numer / total).astype(BF16)

        cross_query = cq_ref[...].astype(F32)
        size = n_rep * slot_rows
        owner_row = lax.broadcasted_iota(jnp.int32, (reqs * group, size), 0) // group
        mask = owner_row == code_ref[...]
        has = jnp.sum(mask.astype(F32), axis=1, keepdims=True) > 0.0
        for d in range(1, n_rep):
            wait_arrival(0, d)
        safe = []
        for h in range(kvh):
            query = cross_query[:, h * group : (h + 1) * group, :]
            query = query.reshape(reqs * group, width).astype(BF16)
            raw = arrived[0, :, :, h * width : (h + 1) * width].astype(F32).reshape(size, width)
            keys = (
                raw * lax.rsqrt(jnp.mean(raw * raw, axis=1, keepdims=True) + 1e-05)
            ).astype(BF16)
            score = (
                lax.dot_general(
                    query, keys, (((1,), (1,)), ((), ())), preferred_element_type=F32
                )
                * scale
            )
            weight = jnp.where(mask, jnp.exp(score), 0.0)
            safe.append(jnp.where(has, jnp.sum(weight, axis=1, keepdims=True), 1.0))
            weights[h] = weight.astype(BF16)
        for d in range(1, n_rep):
            wait_arrival(1, d)
        parts = []
        for h in range(kvh):
            values = arrived[1, :, :, h * width : (h + 1) * width]
            values = values.astype(F32).reshape(size, width).astype(BF16)
            numer = jnp.dot(weights[h], values, preferred_element_type=F32)
            parts.append(jnp.where(has, numer / safe[h], 0.0).reshape(reqs, group, width))
        cross_ref[...] = jnp.concatenate(parts, axis=1).astype(BF16)

        for which in range(2):
            for d in range(1, n_ten):
                to_ten(which, d).wait_send()
            for d in range(1, n_rep):
                to_rep(which, d).wait_send()


def local(
    n_rep,
    n_ten,
    features,
    kv_weight,
    image_owner,
    image_request,
    cross_query,
    self_query,
    self_cache,
    fresh_key_value,
    cache_len,
):
    me = lax.axis_index("replica")
    images, patches, depth = features.shape
    reqs, heads, width = cross_query.shape
    kvh = self_cache.shape[2]
    kvh_all = kv_weight.shape[1]
    group = heads // kvh
    slot_cap = max(2, 2 * images // n_rep)
    rows = images * patches
    slot_rows = slot_cap * patches

    ids = (image_owner * reqs + image_request).reshape(n_rep, images)
    owners = ids // reqs
    mine = lax.dynamic_index_in_dim(ids, me, 0, keepdims=False) // reqs
    at = jnp.arange(images, dtype=jnp.int32)
    earlier = (mine[:, None] == mine[None, :]) & (at[:, None] > at[None, :])
    rank = jnp.sum(earlier.astype(jnp.int32), axis=1, dtype=jnp.int32)
    slot = mine * slot_cap + rank
    slot_row = (slot[:, None] * patches + jnp.arange(patches, dtype=jnp.int32)[None, :]).reshape(
        1, rows
    )

    match = owners == me
    before = (at[:, None] < at[None, :]).astype(BF16)
    place = jnp.dot(match.astype(BF16), before, preferred_element_type=F32).astype(jnp.int32)
    chosen = match[:, None, :] & (
        place[:, None, :] == jnp.arange(slot_cap, dtype=jnp.int32)[None, :, None]
    )
    code = jnp.sum(jnp.where(chosen, (ids - me * reqs)[:, None, :] + 1, 0), axis=-1) - 1
    code = jnp.broadcast_to(code[:, :, None], (n_rep, slot_cap, patches)).reshape(
        1, n_rep * slot_rows
    )

    tile = 256 // kvh_all * kvh_all
    spot = jnp.arange(tile, dtype=jnp.int32)
    origin = (spot % (tile // kvh_all)) * kvh_all + spot // (tile // kvh_all)
    perm = (origin[:, None] == spot[None, :]).astype(BF16)
    fresh = jnp.broadcast_to(
        fresh_key_value[:, :, None, :], (reqs, kvh, group, 2 * width)
    ).reshape(reqs, heads, 2 * width)
    chunk = depth
    for c in range(256, 769, 256):
        if depth % c == 0:
            chunk = c
    steps = depth // chunk
    cols = kvh * width
    vmem = pl.BlockSpec(memory_space=pltpu.VMEM)
    return pl.pallas_call(
        functools.partial(step_kernel, n_rep, n_ten, kvh_all, kvh),
        grid=(2, steps),
        in_specs=[
            pl.BlockSpec(memory_space=pltpu.SMEM),
            vmem,
            vmem,
            vmem,
            pl.BlockSpec(
                (images, patches, chunk), lambda j, k: (0, 0, k * (1 - j) + (steps - 1) * j)
            ),
            pl.BlockSpec((chunk * kvh_all, width), lambda j, k: (k, j)),
            vmem,
            vmem,
            pl.BlockSpec(memory_space=pl.ANY),
            vmem,
        ],
        out_specs=(vmem, vmem),
        out_shape=(
            jax.ShapeDtypeStruct(cross_query.shape, BF16),
            jax.ShapeDtypeStruct(self_query.shape, BF16),
        ),
        scratch_shapes=[
            pltpu.VMEM((steps, rows, chunk), BF16),
            pltpu.VMEM((kvh_all // 2, chunk, 2 * width), BF16),
            pltpu.VMEM((rows, kvh_all * width), F32),
            pltpu.VMEM((2, n_ten, rows, cols), BF16),
            pltpu.VMEM((2, n_ten - 1, rows, cols), BF16),
            pltpu.VMEM((2, n_rep, slot_rows, cols), BF16),
            pltpu.VMEM((2, n_rep, slot_rows, cols), BF16),
            pltpu.VMEM((kvh, reqs * group, n_rep * slot_rows), BF16),
            pltpu.VMEM(self_cache.shape, BF16),
            pltpu.SemaphoreType.DMA,
            pltpu.SemaphoreType.DMA((2, n_ten - 1)),
            pltpu.SemaphoreType.DMA((2, n_ten - 1)),
            pltpu.SemaphoreType.DMA((2, n_rep)),
            pltpu.SemaphoreType.DMA((2, n_rep)),
        ],
        compiler_params=pltpu.CompilerParams(
            collective_id=0,
            has_side_effects=True,
            vmem_limit_bytes=60 * 1024 * 1024,
        ),
    )(
        cache_len,
        slot_row,
        code,
        perm,
        features,
        kv_weight.reshape(depth * kvh_all, 2 * width),
        cross_query,
        self_query,
        self_cache,
        fresh,
    )


def solution(mesh):
    n_rep, n_ten = mesh.shape["replica"], mesh.shape["tensor"]
    return jax.shard_map(
        functools.partial(local, n_rep, n_ten),
        mesh=mesh,
        in_specs=(
            P("replica", None, "tensor"),
            P("tensor", None, None),
            P(),
            P(),
            P("replica", "tensor", None),
            P("replica", "tensor", None),
            P("replica", None, "tensor", None),
            P("replica", "tensor", None),
            P("replica"),
        ),
        out_specs=(P("replica", "tensor", None), P("replica", "tensor", None)),
        check_vma=False,
    )
```

```python
import functools
import math

import jax
import jax.numpy as jnp
from jax import lax
from jax.experimental import pallas as pl
from jax.experimental.pallas import tpu as pltpu
from jax.sharding import PartitionSpec as P

MESH = pl.DeviceIdType.MESH
F32 = jnp.float32
BF16 = jnp.bfloat16


def step_kernel(
    n_rep,
    n_ten,
    kvh_all,
    kvh,
    slot_cap,
    ids_ref,
    len_hbm,
    feat_hbm,
    w_ref,
    cq_hbm,
    sq_hbm,
    cache_hbm,
    fresh_hbm,
    cross_ref,
    self_ref,
    len_ref,
    feat_ref,
    cq_ref,
    sq_ref,
    cache_ref,
    fresh_ref,
    slot_ref,
    code_ref,
    perm_ref,
    feat,
    by_head,
    acc,
    part,
    got,
    outgoing,
    arrived,
    weights,
    feat_sem,
    in_sem,
    send_t,
    recv_t,
    send_r,
    recv_r,
):
    rep = lax.axis_index("replica")
    ten = lax.axis_index("tensor")
    half = pl.program_id(0)
    step = pl.program_id(1)
    steps = pl.num_programs(1)
    reqs, heads, width = cq_ref.shape
    group = heads // kvh
    scale = 1.0 / math.sqrt(width)
    slot_rows = outgoing.shape[2]
    cols = kvh * width
    rows, chunk = feat.shape[1:]
    run = 256 // kvh_all
    tile = run * kvh_all
    patches = slot_rows // slot_cap
    later = [
        pltpu.make_async_copy(source, target, in_sem.at[i])
        for i, (source, target) in enumerate(
            (
                (len_hbm, len_ref),
                (cq_hbm, cq_ref),
                (sq_hbm, sq_ref),
                (cache_hbm, cache_ref),
                (fresh_hbm, fresh_ref),
            )
        )
    ]

    def feat_copy(k):
        if feat_ref.shape[0] == 1:
            source = feat_hbm
        else:
            source = feat_hbm.at[:, :, pl.ds(pl.multiple_of(k * chunk, 128), chunk)]
        return pltpu.make_async_copy(source, feat_ref.at[k], feat_sem.at[k])

    def to_ten(which, d):
        peer = lax.rem(ten + d, n_ten)
        return pltpu.make_async_remote_copy(
            src_ref=part.at[which, peer],
            dst_ref=got.at[which, d - 1],
            send_sem=send_t.at[which, d - 1],
            recv_sem=recv_t.at[which, d - 1],
            device_id=(rep, peer),
            device_id_type=MESH,
        )

    def to_rep(which, d):
        peer = lax.rem(rep + d, n_rep)
        return pltpu.make_async_remote_copy(
            src_ref=outgoing.at[which, peer],
            dst_ref=arrived.at[which, rep],
            send_sem=send_r.at[which, d],
            recv_sem=recv_r.at[which, rep],
            device_id=(peer, ten),
            device_id_type=MESH,
        )

    def wait_arrival(which, d):
        source = lax.rem(rep - d + n_rep, n_rep)
        pltpu.make_async_remote_copy(
            src_ref=outgoing.at[which, source],
            dst_ref=arrived.at[which, source],
            send_sem=send_r.at[which, d],
            recv_sem=recv_r.at[which, source],
            device_id=(source, ten),
            device_id_type=MESH,
        ).wait_recv()

    def route(which):
        at = lax.broadcasted_iota(jnp.int32, (n_rep * slot_rows, rows), 0)
        placing = (at == slot_ref[...]).astype(BF16)
        kv = part[which, ten].astype(F32)
        for d in range(1, n_ten):
            to_ten(which, d).wait_recv()
            kv = kv + got[which, d - 1].astype(F32)
        placed = jnp.dot(placing, kv.astype(BF16), preferred_element_type=F32)
        outgoing[which] = placed.reshape(n_rep, slot_rows, cols).astype(BF16)
        for d in range(1, n_rep):
            to_rep(which, d).start()
        arrived[which, rep] = outgoing[which, rep]

    @pl.when((half == 0) & (step == 0))
    def _():
        barrier = pltpu.get_barrier_semaphore()
        for d in range(1, n_ten):
            peer = lax.rem(ten + d, n_ten)
            pl.semaphore_signal(barrier, inc=1, device_id=(rep, peer), device_id_type=MESH)
        for d in range(1, n_rep):
            peer = lax.rem(rep + d, n_rep)
            pl.semaphore_signal(barrier, inc=1, device_id=(peer, ten), device_id_type=MESH)
        for k in range(feat_ref.shape[0]):
            feat_copy(k).start()
        for copy in later:
            copy.start()
        at = lax.broadcasted_iota(jnp.int32, (tile, tile), 0)
        lane = lax.broadcasted_iota(jnp.int32, (tile, tile), 1)
        perm_ref[...] = (lane == lax.rem(at, run) * kvh_all + at // run).astype(BF16)

        ids = ids_ref[...]
        images = ids.shape[1]
        at = lax.broadcasted_iota(jnp.int32, (images, images), 0)
        lane = lax.broadcasted_iota(jnp.int32, (images, images), 1)
        mine = (ids_ref[pl.ds(rep, 1), :] // reqs).astype(F32)
        mine_col = jnp.sum(jnp.where(at == lane, mine, 0.0), axis=1, keepdims=True)
        earlier = (mine_col == mine) & (lane < at)
        rank = jnp.sum(jnp.where(earlier, 1.0, 0.0), axis=1, keepdims=True)
        slot = (mine_col * slot_cap + rank) * patches
        at_row = lax.broadcasted_iota(jnp.int32, (images, rows), 0)
        lane_row = lax.broadcasted_iota(jnp.int32, (images, rows), 1)
        slot = jnp.where(
            at_row == lane_row // patches, slot + lax.rem(lane_row, patches).astype(F32), 0.0
        )
        slot_ref[...] = jnp.sum(slot, axis=0, keepdims=True).astype(jnp.int32)

        match = ids // reqs == rep
        before = (at < lane).astype(BF16)
        place = jnp.dot(
            jnp.where(match, 1.0, 0.0).astype(BF16), before, preferred_element_type=F32
        )
        size = n_rep * slot_rows
        pick = (
            lax.broadcasted_iota(jnp.int32, (size, n_rep), 1)
            == lax.broadcasted_iota(jnp.int32, (size, n_rep), 0) // slot_rows
        ).astype(BF16)
        placed = jnp.dot(
            pick, jnp.where(match, place + 1.0, 0.0).astype(BF16), preferred_element_type=F32
        )
        asked = jnp.where(match, (lax.rem(ids, reqs) + 1).astype(F32), 0.0)
        asked = jnp.dot(pick, asked.astype(BF16), preferred_element_type=F32)
        at = lax.broadcasted_iota(jnp.int32, (size, images), 0)
        want = (lax.rem(at, slot_rows) // patches + 1).astype(F32)
        code = jnp.sum(jnp.where(placed == want, asked, 0.0), axis=1, keepdims=True) - 1.0
        for first in range(0, size, 128):
            at = lax.broadcasted_iota(jnp.int32, (128, 128), 0)
            lane = lax.broadcasted_iota(jnp.int32, (128, 128), 1)
            turned = jnp.where(at == lane, code[first : first + 128], 0.0)
            code_ref[:, first : first + 128] = jnp.sum(turned, axis=0, keepdims=True).astype(
                jnp.int32
            )

    @pl.when(half == 0)
    def _():
        feat_copy(step).wait()
        feat[step] = feat_ref[step].astype(F32).reshape(rows, chunk).astype(BF16)

    @pl.when(step == 0)
    def _():
        acc[...] = jnp.zeros_like(acc)

    perm = perm_ref[...]
    for g in range(0, chunk // run, 2):
        two = jnp.concatenate(
            [w_ref[g * tile : (g + 1) * tile, :], w_ref[(g + 1) * tile : (g + 2) * tile, :]],
            axis=1,
        )
        moved = jnp.dot(perm, two, preferred_element_type=F32).astype(BF16)
        for h in range(kvh_all):
            lanes = (h % 2) * width
            for q in range(2):
                by_head[
                    h // 2, (g + q) * run : (g + q + 1) * run, lanes : lanes + width
                ] = moved[h * run : (h + 1) * run, q * width : (q + 1) * width]
    now = feat[step]
    for p in range(kvh_all // 2):
        acc[:, p * 2 * width : (p + 1) * 2 * width] += jnp.dot(
            now, by_head[p], preferred_element_type=F32
        )

    @pl.when(step == steps - 1)
    def _():
        for t in range(n_ten):
            part[half, t] = acc[:, t * cols : (t + 1) * cols].astype(BF16)

    @pl.when((half == 0) & (step == steps - 1))
    def _():
        pl.semaphore_wait(pltpu.get_barrier_semaphore(), n_ten + n_rep - 2)
        for d in range(1, n_ten):
            to_ten(0, d).start()

    @pl.when((half == 1) & (step == jnp.minimum(1, steps - 1)))
    def _():
        route(0)

    @pl.when((half == 1) & (step == steps - 1))
    def _():
        for d in range(1, n_ten):
            to_ten(1, d).start()
        route(1)

        for copy in later:
            copy.wait()
        places = cache_ref.shape[1] * kvh
        col = lax.broadcasted_iota(jnp.int32, (heads, places), 1)
        row = lax.broadcasted_iota(jnp.int32, (heads, places), 0)
        same_head = lax.rem(col, kvh) == row // group
        for b in range(reqs):
            query = sq_ref[b]
            both = cache_ref[b].astype(F32).reshape(places, 2 * width).astype(BF16)
            score = (
                lax.dot_general(
                    query, both[:, :width], (((1,), (1,)), ((), ())), preferred_element_type=F32
                )
                * scale
            )
            live = same_head & (col // kvh < len_ref[b])
            weight = jnp.where(live, jnp.exp(score), 0.0)
            fresh = jnp.broadcast_to(
                fresh_ref[b].astype(F32)[:, None, :], (kvh, group, 2 * width)
            ).reshape(heads, 2 * width)
            fresh_weight = jnp.exp(
                jnp.sum(query.astype(F32) * fresh[:, :width], axis=1, keepdims=True) * scale
            )
            total = jnp.sum(weight, axis=1, keepdims=True) + fresh_weight
            numer = jnp.dot(
                weight.astype(BF16), both[:, width:], preferred_element_type=F32
            )
            numer = numer + fresh_weight.astype(BF16).astype(F32) * fresh[:, width:]
            self_ref[b] = (numer / total).astype(BF16)

        cross_query = cq_ref[...].astype(F32)
        size = n_rep * slot_rows
        owner_row = lax.broadcasted_iota(jnp.int32, (reqs * group, size), 0) // group
        mask = owner_row == code_ref[...]
        has = jnp.sum(mask.astype(F32), axis=1, keepdims=True) > 0.0
        for d in range(1, n_rep):
            wait_arrival(0, d)
        safe = []
        for h in range(kvh):
            query = cross_query[:, h * group : (h + 1) * group, :]
            query = query.reshape(reqs * group, width).astype(BF16)
            raw = arrived[0, :, :, h * width : (h + 1) * width].astype(F32).reshape(size, width)
            keys = (
                raw * lax.rsqrt(jnp.mean(raw * raw, axis=1, keepdims=True) + 1e-05)
            ).astype(BF16)
            score = (
                lax.dot_general(
                    query, keys, (((1,), (1,)), ((), ())), preferred_element_type=F32
                )
                * scale
            )
            weight = jnp.where(mask, jnp.exp(score), 0.0)
            safe.append(jnp.where(has, jnp.sum(weight, axis=1, keepdims=True), 1.0))
            weights[h] = weight.astype(BF16)
        for d in range(1, n_rep):
            wait_arrival(1, d)
        parts = []
        for h in range(kvh):
            values = arrived[1, :, :, h * width : (h + 1) * width]
            values = values.astype(F32).reshape(size, width).astype(BF16)
            numer = jnp.dot(weights[h], values, preferred_element_type=F32)
            parts.append(jnp.where(has, numer / safe[h], 0.0).reshape(reqs, group, width))
        cross_ref[...] = jnp.concatenate(parts, axis=1).astype(BF16)

        for which in range(2):
            for d in range(1, n_ten):
                to_ten(which, d).wait_send()
            for d in range(1, n_rep):
                to_rep(which, d).wait_send()


def local(
    n_rep,
    n_ten,
    features,
    kv_weight,
    image_owner,
    image_request,
    cross_query,
    self_query,
    self_cache,
    fresh_key_value,
    cache_len,
):
    images, patches, depth = features.shape
    reqs, heads, width = cross_query.shape
    kvh = self_cache.shape[2]
    kvh_all = kv_weight.shape[1]
    group = heads // kvh
    slot_cap = max(2, 2 * images // n_rep)
    rows = images * patches
    slot_rows = slot_cap * patches

    ids = (image_owner * reqs + image_request).reshape(n_rep, images)
    chunk = depth
    for c in range(256, 769, 256):
        if depth % c == 0:
            chunk = c
    steps = depth // chunk
    cols = kvh * width
    tile = 256 // kvh_all * kvh_all
    vmem = pl.BlockSpec(memory_space=pltpu.VMEM)
    hbm = pl.BlockSpec(memory_space=pltpu.HBM)
    return pl.pallas_call(
        functools.partial(step_kernel, n_rep, n_ten, kvh_all, kvh, slot_cap),
        grid=(2, steps),
        in_specs=[
            vmem,
            hbm,
            hbm,
            pl.BlockSpec((chunk * kvh_all, width), lambda j, k: (k, j)),
            hbm,
            hbm,
            hbm,
            hbm,
        ],
        out_specs=(vmem, vmem),
        out_shape=(
            jax.ShapeDtypeStruct(cross_query.shape, BF16),
            jax.ShapeDtypeStruct(self_query.shape, BF16),
        ),
        scratch_shapes=[
            pltpu.SMEM(cache_len.shape, jnp.int32),
            pltpu.VMEM((steps, images, patches, chunk), BF16),
            pltpu.VMEM(cross_query.shape, BF16),
            pltpu.VMEM(self_query.shape, BF16),
            pltpu.VMEM(self_cache.shape, BF16),
            pltpu.VMEM(fresh_key_value.shape, BF16),
            pltpu.VMEM((1, rows), jnp.int32),
            pltpu.VMEM((1, n_rep * slot_rows), jnp.int32),
            pltpu.VMEM((tile, tile), BF16),
            pltpu.VMEM((steps, rows, chunk), BF16),
            pltpu.VMEM((kvh_all // 2, chunk, 2 * width), BF16),
            pltpu.VMEM((rows, kvh_all * width), F32),
            pltpu.VMEM((2, n_ten, rows, cols), BF16),
            pltpu.VMEM((2, n_ten - 1, rows, cols), BF16),
            pltpu.VMEM((2, n_rep, slot_rows, cols), BF16),
            pltpu.VMEM((2, n_rep, slot_rows, cols), BF16),
            pltpu.VMEM((kvh, reqs * group, n_rep * slot_rows), BF16),
            pltpu.SemaphoreType.DMA((steps,)),
            pltpu.SemaphoreType.DMA((5,)),
            pltpu.SemaphoreType.DMA((2, n_ten - 1)),
            pltpu.SemaphoreType.DMA((2, n_ten - 1)),
            pltpu.SemaphoreType.DMA((2, n_rep)),
            pltpu.SemaphoreType.DMA((2, n_rep)),
        ],
        compiler_params=pltpu.CompilerParams(
            collective_id=0,
            has_side_effects=True,
            vmem_limit_bytes=60 * 1024 * 1024,
        ),
    )(
        ids,
        cache_len,
        features,
        kv_weight.reshape(depth * kvh_all, 2 * width),
        cross_query,
        self_query,
        self_cache,
        fresh_key_value,
    )


def solution(mesh):
    n_rep, n_ten = mesh.shape["replica"], mesh.shape["tensor"]
    return jax.shard_map(
        functools.partial(local, n_rep, n_ten),
        mesh=mesh,
        in_specs=(
            P("replica", None, "tensor"),
            P("tensor", None, None),
            P(),
            P(),
            P("replica", "tensor", None),
            P("replica", "tensor", None),
            P("replica", None, "tensor", None),
            P("replica", "tensor", None),
            P("replica"),
        ),
        out_specs=(P("replica", "tensor", None), P("replica", "tensor", None)),
        check_vma=False,
    )
```

```python
import functools
import math

import jax
import jax.numpy as jnp
from jax import lax
from jax.experimental import pallas as pl
from jax.experimental.pallas import tpu as pltpu
from jax.sharding import PartitionSpec as P

MESH = pl.DeviceIdType.MESH
F32 = jnp.float32
BF16 = jnp.bfloat16


def step_kernel(
    n_rep,
    n_ten,
    kvh_all,
    kvh,
    slot_cap,
    owner_ref,
    request_ref,
    len_hbm,
    feat_hbm,
    w_ref,
    cq_hbm,
    sq_hbm,
    cache_hbm,
    fresh_hbm,
    cross_ref,
    self_ref,
    len_ref,
    feat_ref,
    cq_ref,
    sq_ref,
    cache_ref,
    fresh_ref,
    ids_ref,
    slot_ref,
    code_ref,
    perm_ref,
    feat,
    by_head,
    acc,
    part,
    got,
    outgoing,
    arrived,
    weights,
    feat_sem,
    in_sem,
    send_t,
    recv_t,
    send_r,
    recv_r,
):
    rep = lax.axis_index("replica")
    ten = lax.axis_index("tensor")
    half = pl.program_id(0)
    step = pl.program_id(1)
    steps = pl.num_programs(1)
    reqs, heads, width = cq_ref.shape
    group = heads // kvh
    scale = 1.0 / math.sqrt(width)
    slot_rows = outgoing.shape[2]
    cols = kvh * width
    rows, chunk = feat.shape[1:]
    run = 256 // kvh_all
    tile = run * kvh_all
    patches = slot_rows // slot_cap
    later = [
        pltpu.make_async_copy(source, target, in_sem.at[i])
        for i, (source, target) in enumerate(
            (
                (len_hbm, len_ref),
                (cq_hbm, cq_ref),
                (sq_hbm, sq_ref),
                (cache_hbm, cache_ref),
                (fresh_hbm, fresh_ref),
            )
        )
    ]

    def feat_copy(k):
        if feat_ref.shape[0] == 1:
            source = feat_hbm
        else:
            source = feat_hbm.at[:, :, pl.ds(pl.multiple_of(k * chunk, 128), chunk)]
        return pltpu.make_async_copy(source, feat_ref.at[k], feat_sem.at[k])

    def to_ten(which, d):
        peer = lax.rem(ten + d, n_ten)
        return pltpu.make_async_remote_copy(
            src_ref=part.at[which, peer],
            dst_ref=got.at[which, d - 1],
            send_sem=send_t.at[which, d - 1],
            recv_sem=recv_t.at[which, d - 1],
            device_id=(rep, peer),
            device_id_type=MESH,
        )

    def to_rep(which, d):
        peer = lax.rem(rep + d, n_rep)
        return pltpu.make_async_remote_copy(
            src_ref=outgoing.at[which, peer],
            dst_ref=arrived.at[which, rep],
            send_sem=send_r.at[which, d],
            recv_sem=recv_r.at[which, rep],
            device_id=(peer, ten),
            device_id_type=MESH,
        )

    def wait_arrival(which, d):
        source = lax.rem(rep - d + n_rep, n_rep)
        pltpu.make_async_remote_copy(
            src_ref=outgoing.at[which, source],
            dst_ref=arrived.at[which, source],
            send_sem=send_r.at[which, d],
            recv_sem=recv_r.at[which, source],
            device_id=(source, ten),
            device_id_type=MESH,
        ).wait_recv()

    def route(which):
        at = lax.broadcasted_iota(jnp.int32, (n_rep * slot_rows, rows), 0)
        placing = (at == slot_ref[...]).astype(BF16)
        kv = part[which, ten].astype(F32)
        for d in range(1, n_ten):
            to_ten(which, d).wait_recv()
            kv = kv + got[which, d - 1].astype(F32)
        placed = jnp.dot(placing, kv.astype(BF16), preferred_element_type=F32)
        outgoing[which] = placed.reshape(n_rep, slot_rows, cols).astype(BF16)
        for d in sorted(range(1, n_rep), key=lambda d: abs(d - n_rep // 2)):
            to_rep(which, d).start()
        arrived[which, rep] = outgoing[which, rep]

    @pl.when((half == 0) & (step == 0))
    def _():
        barrier = pltpu.get_barrier_semaphore()
        for d in range(1, n_ten):
            peer = lax.rem(ten + d, n_ten)
            pl.semaphore_signal(barrier, inc=1, device_id=(rep, peer), device_id_type=MESH)
        for d in range(1, n_rep):
            peer = lax.rem(rep + d, n_rep)
            pl.semaphore_signal(barrier, inc=1, device_id=(peer, ten), device_id_type=MESH)
        for k in range(feat_ref.shape[0]):
            feat_copy(k).start()
        for copy in later:
            copy.start()
        at = lax.broadcasted_iota(jnp.int32, (tile, tile), 0)
        lane = lax.broadcasted_iota(jnp.int32, (tile, tile), 1)
        perm_ref[...] = (lane == lax.rem(at, run) * kvh_all + at // run).astype(BF16)

        images = ids_ref.shape[1]
        lanes = owner_ref.shape[1]
        for b in range(n_rep):
            r, c = divmod(b * images, lanes)
            ids_ref[b : b + 1, :] = (
                owner_ref[r : r + 1, c : c + images] * reqs
                + request_ref[r : r + 1, c : c + images]
            )
        ids = ids_ref[...]
        at = lax.broadcasted_iota(jnp.int32, (images, images), 0)
        lane = lax.broadcasted_iota(jnp.int32, (images, images), 1)
        mine = (ids_ref[pl.ds(rep, 1), :] // reqs).astype(F32)
        mine_col = jnp.sum(jnp.where(at == lane, mine, 0.0), axis=1, keepdims=True)
        earlier = (mine_col == mine) & (lane < at)
        rank = jnp.sum(jnp.where(earlier, 1.0, 0.0), axis=1, keepdims=True)
        slot = (mine_col * slot_cap + rank) * patches
        at_row = lax.broadcasted_iota(jnp.int32, (images, rows), 0)
        lane_row = lax.broadcasted_iota(jnp.int32, (images, rows), 1)
        slot = jnp.where(
            at_row == lane_row // patches, slot + lax.rem(lane_row, patches).astype(F32), 0.0
        )
        slot_ref[...] = jnp.sum(slot, axis=0, keepdims=True).astype(jnp.int32)

        match = ids // reqs == rep
        before = (at < lane).astype(BF16)
        place = jnp.dot(
            jnp.where(match, 1.0, 0.0).astype(BF16), before, preferred_element_type=F32
        )
        size = n_rep * slot_rows
        pick = (
            lax.broadcasted_iota(jnp.int32, (size, n_rep), 1)
            == lax.broadcasted_iota(jnp.int32, (size, n_rep), 0) // slot_rows
        ).astype(BF16)
        placed = jnp.dot(
            pick, jnp.where(match, place + 1.0, 0.0).astype(BF16), preferred_element_type=F32
        )
        asked = jnp.where(match, (lax.rem(ids, reqs) + 1).astype(F32), 0.0)
        asked = jnp.dot(pick, asked.astype(BF16), preferred_element_type=F32)
        at = lax.broadcasted_iota(jnp.int32, (size, images), 0)
        want = (lax.rem(at, slot_rows) // patches + 1).astype(F32)
        code = jnp.sum(jnp.where(placed == want, asked, 0.0), axis=1, keepdims=True) - 1.0
        for first in range(0, size, 128):
            at = lax.broadcasted_iota(jnp.int32, (128, 128), 0)
            lane = lax.broadcasted_iota(jnp.int32, (128, 128), 1)
            turned = jnp.where(at == lane, code[first : first + 128], 0.0)
            code_ref[:, first : first + 128] = jnp.sum(turned, axis=0, keepdims=True).astype(
                jnp.int32
            )

    @pl.when(half == 0)
    def _():
        feat_copy(step).wait()
        feat[step] = feat_ref[step].astype(F32).reshape(rows, chunk).astype(BF16)

    @pl.when(step == 0)
    def _():
        acc[...] = jnp.zeros_like(acc)

    perm = perm_ref[...]
    for g in range(0, chunk // run, 2):
        two = jnp.concatenate(
            [w_ref[g * tile : (g + 1) * tile, :], w_ref[(g + 1) * tile : (g + 2) * tile, :]],
            axis=1,
        )
        moved = jnp.dot(perm, two, preferred_element_type=F32).astype(BF16)
        for h in range(kvh_all):
            lanes = (h % 2) * width
            for q in range(2):
                by_head[
                    h // 2, (g + q) * run : (g + q + 1) * run, lanes : lanes + width
                ] = moved[h * run : (h + 1) * run, q * width : (q + 1) * width]
    now = feat[step]
    for p in range(kvh_all // 2):
        acc[:, p * 2 * width : (p + 1) * 2 * width] += jnp.dot(
            now, by_head[p], preferred_element_type=F32
        )

    @pl.when(step == steps - 1)
    def _():
        for t in range(n_ten):
            part[half, t] = acc[:, t * cols : (t + 1) * cols].astype(BF16)

    @pl.when((half == 0) & (step == steps - 1))
    def _():
        pl.semaphore_wait(pltpu.get_barrier_semaphore(), n_ten + n_rep - 2)
        for d in range(1, n_ten):
            to_ten(0, d).start()

    @pl.when((half == 1) & (step == 0))
    def _():
        route(0)

    @pl.when((half == 1) & (step == steps - 1))
    def _():
        for d in range(1, n_ten):
            to_ten(1, d).start()
        route(1)

        for copy in later:
            copy.wait()
        places = cache_ref.shape[1] * kvh
        col = lax.broadcasted_iota(jnp.int32, (heads, places), 1)
        row = lax.broadcasted_iota(jnp.int32, (heads, places), 0)
        same_head = lax.rem(col, kvh) == row // group
        for b in range(reqs):
            query = sq_ref[b]
            both = cache_ref[b].astype(F32).reshape(places, 2 * width).astype(BF16)
            score = (
                lax.dot_general(
                    query, both[:, :width], (((1,), (1,)), ((), ())), preferred_element_type=F32
                )
                * scale
            )
            live = same_head & (col // kvh < len_ref[b])
            weight = jnp.where(live, jnp.exp(score), 0.0)
            fresh = jnp.broadcast_to(
                fresh_ref[b].astype(F32)[:, None, :], (kvh, group, 2 * width)
            ).reshape(heads, 2 * width)
            fresh_weight = jnp.exp(
                jnp.sum(query.astype(F32) * fresh[:, :width], axis=1, keepdims=True) * scale
            )
            total = jnp.sum(weight, axis=1, keepdims=True) + fresh_weight
            numer = jnp.dot(
                weight.astype(BF16), both[:, width:], preferred_element_type=F32
            )
            numer = numer + fresh_weight.astype(BF16).astype(F32) * fresh[:, width:]
            self_ref[b] = (numer / total).astype(BF16)

        cross_query = cq_ref[...].astype(F32)
        size = n_rep * slot_rows
        owner_row = lax.broadcasted_iota(jnp.int32, (reqs * group, size), 0) // group
        mask = owner_row == code_ref[...]
        has = jnp.sum(mask.astype(F32), axis=1, keepdims=True) > 0.0
        for d in range(1, n_rep):
            wait_arrival(0, d)
        safe = []
        for h in range(kvh):
            query = cross_query[:, h * group : (h + 1) * group, :]
            query = query.reshape(reqs * group, width).astype(BF16)
            raw = arrived[0, :, :, h * width : (h + 1) * width].astype(F32).reshape(size, width)
            keys = (
                raw * lax.rsqrt(jnp.mean(raw * raw, axis=1, keepdims=True) + 1e-05)
            ).astype(BF16)
            score = (
                lax.dot_general(
                    query, keys, (((1,), (1,)), ((), ())), preferred_element_type=F32
                )
                * scale
            )
            weight = jnp.where(mask, jnp.exp(score), 0.0)
            safe.append(jnp.where(has, jnp.sum(weight, axis=1, keepdims=True), 1.0))
            weights[h] = weight.astype(BF16)
        for d in range(1, n_rep):
            wait_arrival(1, d)
        parts = []
        for h in range(kvh):
            values = arrived[1, :, :, h * width : (h + 1) * width]
            values = values.astype(F32).reshape(size, width).astype(BF16)
            numer = jnp.dot(weights[h], values, preferred_element_type=F32)
            parts.append(jnp.where(has, numer / safe[h], 0.0).reshape(reqs, group, width))
        cross_ref[...] = jnp.concatenate(parts, axis=1).astype(BF16)

        for which in range(2):
            for d in range(1, n_ten):
                to_ten(which, d).wait_send()
            for d in range(1, n_rep):
                to_rep(which, d).wait_send()


def hand_out_kernel(cross_in, self_in, cross_out, self_out, sems):
    first = pltpu.make_async_copy(cross_in, cross_out, sems.at[0])
    second = pltpu.make_async_copy(self_in, self_out, sems.at[1])
    first.start()
    second.start()
    first.wait()
    second.wait()


def local(
    n_rep,
    n_ten,
    features,
    kv_weight,
    image_owner,
    image_request,
    cross_query,
    self_query,
    self_cache,
    fresh_key_value,
    cache_len,
):
    images, patches, depth = features.shape
    reqs, heads, width = cross_query.shape
    kvh = self_cache.shape[2]
    kvh_all = kv_weight.shape[1]
    group = heads // kvh
    slot_cap = max(2, 2 * images // n_rep)
    rows = images * patches
    slot_rows = slot_cap * patches

    lanes = 128 // math.gcd(128, images) * images
    chunk = depth
    for c in range(256, 769, 256):
        if depth % c == 0:
            chunk = c
    steps = depth // chunk
    cols = kvh * width
    tile = 256 // kvh_all * kvh_all
    vmem = pl.BlockSpec(memory_space=pltpu.VMEM)
    hbm = pl.BlockSpec(memory_space=pltpu.HBM)
    cross, own = pl.pallas_call(
        functools.partial(step_kernel, n_rep, n_ten, kvh_all, kvh, slot_cap),
        grid=(2, steps),
        in_specs=[
            vmem,
            vmem,
            hbm,
            hbm,
            pl.BlockSpec((chunk * kvh_all, width), lambda j, k: (k, j)),
            hbm,
            hbm,
            hbm,
            hbm,
        ],
        out_specs=(vmem, vmem),
        out_shape=(
            jax.ShapeDtypeStruct(cross_query.shape, BF16),
            jax.ShapeDtypeStruct(self_query.shape, BF16),
        ),
        scratch_shapes=[
            pltpu.SMEM(cache_len.shape, jnp.int32),
            pltpu.VMEM((steps, images, patches, chunk), BF16),
            pltpu.VMEM(cross_query.shape, BF16),
            pltpu.VMEM(self_query.shape, BF16),
            pltpu.VMEM(self_cache.shape, BF16),
            pltpu.VMEM(fresh_key_value.shape, BF16),
            pltpu.VMEM((n_rep, images), jnp.int32),
            pltpu.VMEM((1, rows), jnp.int32),
            pltpu.VMEM((1, n_rep * slot_rows), jnp.int32),
            pltpu.VMEM((tile, tile), BF16),
            pltpu.VMEM((steps, rows, chunk), BF16),
            pltpu.VMEM((kvh_all // 2, chunk, 2 * width), BF16),
            pltpu.VMEM((rows, kvh_all * width), F32),
            pltpu.VMEM((2, n_ten, rows, cols), BF16),
            pltpu.VMEM((2, n_ten - 1, rows, cols), BF16),
            pltpu.VMEM((2, n_rep, slot_rows, cols), BF16),
            pltpu.VMEM((2, n_rep, slot_rows, cols), BF16),
            pltpu.VMEM((kvh, reqs * group, n_rep * slot_rows), BF16),
            pltpu.SemaphoreType.DMA((steps,)),
            pltpu.SemaphoreType.DMA((5,)),
            pltpu.SemaphoreType.DMA((2, n_ten - 1)),
            pltpu.SemaphoreType.DMA((2, n_ten - 1)),
            pltpu.SemaphoreType.DMA((2, n_rep)),
            pltpu.SemaphoreType.DMA((2, n_rep)),
        ],
        compiler_params=pltpu.CompilerParams(
            collective_id=0,
            has_side_effects=True,
            vmem_limit_bytes=60 * 1024 * 1024,
        ),
    )(
        image_owner.reshape(n_rep * images // lanes, lanes),
        image_request.reshape(n_rep * images // lanes, lanes),
        cache_len,
        features,
        kv_weight.reshape(depth * kvh_all, 2 * width),
        cross_query,
        self_query,
        self_cache,
        fresh_key_value,
    )
    anywhere = pl.BlockSpec(memory_space=pl.ANY)
    return pl.pallas_call(
        hand_out_kernel,
        in_specs=[anywhere, anywhere],
        out_specs=(anywhere, anywhere),
        out_shape=(
            jax.ShapeDtypeStruct(cross.shape, BF16),
            jax.ShapeDtypeStruct(own.shape, BF16),
        ),
        scratch_shapes=[pltpu.SemaphoreType.DMA((2,))],
        compiler_params=pltpu.CompilerParams(vmem_limit_bytes=60 * 1024 * 1024),
    )(cross, own)


def solution(mesh):
    n_rep, n_ten = mesh.shape["replica"], mesh.shape["tensor"]
    return jax.shard_map(
        functools.partial(local, n_rep, n_ten),
        mesh=mesh,
        in_specs=(
            P("replica", None, "tensor"),
            P("tensor", None, None),
            P(),
            P(),
            P("replica", "tensor", None),
            P("replica", "tensor", None),
            P("replica", None, "tensor", None),
            P("replica", "tensor", None),
            P("replica"),
        ),
        out_specs=(P("replica", "tensor", None), P("replica", "tensor", None)),
        check_vma=False,
    )
```

```python
import functools
import math

import jax
import jax.numpy as jnp
from jax import lax
from jax.experimental import pallas as pl
from jax.experimental.pallas import tpu as pltpu
from jax.sharding import PartitionSpec as P

MESH = pl.DeviceIdType.MESH
F32 = jnp.float32
BF16 = jnp.bfloat16


def step_kernel(
    n_rep,
    n_ten,
    kvh_all,
    kvh,
    slot_cap,
    owner_ref,
    request_ref,
    len_hbm,
    feat_hbm,
    w_ref,
    cq_hbm,
    sq_hbm,
    cache_hbm,
    fresh_hbm,
    cross_ref,
    self_ref,
    len_ref,
    feat_ref,
    cq_ref,
    sq_ref,
    cache_ref,
    fresh_ref,
    ids_ref,
    slot_ref,
    code_ref,
    perm_ref,
    feat,
    by_head,
    acc,
    part,
    got,
    outgoing,
    arrived,
    weights,
    feat_sem,
    in_sem,
    send_t,
    recv_t,
    send_r,
    recv_r,
):
    rep = lax.axis_index("replica")
    ten = lax.axis_index("tensor")
    half = pl.program_id(0)
    step = pl.program_id(1)
    steps = pl.num_programs(1)
    reqs, heads, width = cq_ref.shape
    group = heads // kvh
    scale = 1.0 / math.sqrt(width)
    slot_rows = outgoing.shape[2]
    cols = kvh * width
    rows, chunk = feat.shape[1:]
    run = 256 // kvh_all
    tile = run * kvh_all
    patches = slot_rows // slot_cap
    later = [
        pltpu.make_async_copy(source, target, in_sem.at[i])
        for i, (source, target) in enumerate(
            (
                (len_hbm, len_ref),
                (cq_hbm, cq_ref),
                (sq_hbm, sq_ref),
                (cache_hbm, cache_ref),
                (fresh_hbm, fresh_ref),
            )
        )
    ]

    def feat_copy(k):
        if feat_ref.shape[0] == 1:
            source = feat_hbm
        else:
            source = feat_hbm.at[:, :, pl.ds(pl.multiple_of(k * chunk, 128), chunk)]
        return pltpu.make_async_copy(source, feat_ref.at[k], feat_sem.at[k])

    def to_ten(which, d):
        peer = lax.rem(ten + d, n_ten)
        return pltpu.make_async_remote_copy(
            src_ref=part.at[which, peer],
            dst_ref=got.at[which, d - 1],
            send_sem=send_t.at[which, d - 1],
            recv_sem=recv_t.at[which, d - 1],
            device_id=(rep, peer),
            device_id_type=MESH,
        )

    def to_rep(which, d):
        peer = lax.rem(rep + d, n_rep)
        return pltpu.make_async_remote_copy(
            src_ref=outgoing.at[which, peer],
            dst_ref=arrived.at[which, rep],
            send_sem=send_r.at[which, d],
            recv_sem=recv_r.at[which, rep],
            device_id=(peer, ten),
            device_id_type=MESH,
        )

    def wait_arrival(which, d):
        source = lax.rem(rep - d + n_rep, n_rep)
        pltpu.make_async_remote_copy(
            src_ref=outgoing.at[which, source],
            dst_ref=arrived.at[which, source],
            send_sem=send_r.at[which, d],
            recv_sem=recv_r.at[which, source],
            device_id=(source, ten),
            device_id_type=MESH,
        ).wait_recv()

    def route(which):
        at = lax.broadcasted_iota(jnp.int32, (n_rep * slot_rows, rows), 0)
        placing = (at == slot_ref[...]).astype(BF16)
        kv = part[which, ten].astype(F32)
        for d in range(1, n_ten):
            to_ten(which, d).wait_recv()
            kv = kv + got[which, d - 1].astype(F32)
        placed = jnp.dot(placing, kv.astype(BF16), preferred_element_type=F32)
        outgoing[which] = placed.reshape(n_rep, slot_rows, cols).astype(BF16)
        for d in range(1, n_rep):
            to_rep(which, d).start()
        arrived[which, rep] = outgoing[which, rep]

    @pl.when((half == 0) & (step == 0))
    def _():
        barrier = pltpu.get_barrier_semaphore()
        for d in range(1, n_ten):
            peer = lax.rem(ten + d, n_ten)
            pl.semaphore_signal(barrier, inc=1, device_id=(rep, peer), device_id_type=MESH)
        for d in range(1, n_rep):
            peer = lax.rem(rep + d, n_rep)
            pl.semaphore_signal(barrier, inc=1, device_id=(peer, ten), device_id_type=MESH)
        for k in range(feat_ref.shape[0]):
            feat_copy(k).start()
        for copy in later:
            copy.start()
        at = lax.broadcasted_iota(jnp.int32, (tile, tile), 0)
        lane = lax.broadcasted_iota(jnp.int32, (tile, tile), 1)
        perm_ref[...] = (lane == lax.rem(at, run) * kvh_all + at // run).astype(BF16)

        images = ids_ref.shape[1]
        lanes = owner_ref.shape[1]
        for b in range(n_rep):
            r, c = divmod(b * images, lanes)
            ids_ref[b : b + 1, :] = (
                owner_ref[r : r + 1, c : c + images] * reqs
                + request_ref[r : r + 1, c : c + images]
            )
        ids = ids_ref[...]
        at = lax.broadcasted_iota(jnp.int32, (images, images), 0)
        lane = lax.broadcasted_iota(jnp.int32, (images, images), 1)
        mine = (ids_ref[pl.ds(rep, 1), :] // reqs).astype(F32)
        mine_col = jnp.sum(jnp.where(at == lane, mine, 0.0), axis=1, keepdims=True)
        earlier = (mine_col == mine) & (lane < at)
        rank = jnp.sum(jnp.where(earlier, 1.0, 0.0), axis=1, keepdims=True)
        slot = (mine_col * slot_cap + rank) * patches
        at_row = lax.broadcasted_iota(jnp.int32, (images, rows), 0)
        lane_row = lax.broadcasted_iota(jnp.int32, (images, rows), 1)
        slot = jnp.where(
            at_row == lane_row // patches, slot + lax.rem(lane_row, patches).astype(F32), 0.0
        )
        slot_ref[...] = jnp.sum(slot, axis=0, keepdims=True).astype(jnp.int32)

        match = ids // reqs == rep
        before = (at < lane).astype(BF16)
        place = jnp.dot(
            jnp.where(match, 1.0, 0.0).astype(BF16), before, preferred_element_type=F32
        )
        size = n_rep * slot_rows
        pick = (
            lax.broadcasted_iota(jnp.int32, (size, n_rep), 1)
            == lax.broadcasted_iota(jnp.int32, (size, n_rep), 0) // slot_rows
        ).astype(BF16)
        placed = jnp.dot(
            pick, jnp.where(match, place + 1.0, 0.0).astype(BF16), preferred_element_type=F32
        )
        asked = jnp.where(match, (lax.rem(ids, reqs) + 1).astype(F32), 0.0)
        asked = jnp.dot(pick, asked.astype(BF16), preferred_element_type=F32)
        at = lax.broadcasted_iota(jnp.int32, (size, images), 0)
        want = (lax.rem(at, slot_rows) // patches + 1).astype(F32)
        code = jnp.sum(jnp.where(placed == want, asked, 0.0), axis=1, keepdims=True) - 1.0
        for first in range(0, size, 128):
            at = lax.broadcasted_iota(jnp.int32, (128, 128), 0)
            lane = lax.broadcasted_iota(jnp.int32, (128, 128), 1)
            turned = jnp.where(at == lane, code[first : first + 128], 0.0)
            code_ref[:, first : first + 128] = jnp.sum(turned, axis=0, keepdims=True).astype(
                jnp.int32
            )

    @pl.when(half == 0)
    def _():
        feat_copy(step).wait()
        feat[step] = feat_ref[step].astype(F32).reshape(rows, chunk).astype(BF16)

    @pl.when(step == 0)
    def _():
        acc[...] = jnp.zeros_like(acc)

    perm = perm_ref[...]
    for g in range(0, chunk // run, 2):
        two = jnp.concatenate(
            [w_ref[g * tile : (g + 1) * tile, :], w_ref[(g + 1) * tile : (g + 2) * tile, :]],
            axis=1,
        )
        moved = jnp.dot(perm, two, preferred_element_type=F32).astype(BF16)
        for h in range(kvh_all):
            lanes = (h % 2) * width
            for q in range(2):
                by_head[
                    h // 2, (g + q) * run : (g + q + 1) * run, lanes : lanes + width
                ] = moved[h * run : (h + 1) * run, q * width : (q + 1) * width]
    now = feat[step]
    for p in range(kvh_all // 2):
        acc[:, p * 2 * width : (p + 1) * 2 * width] += jnp.dot(
            now, by_head[p], preferred_element_type=F32
        )

    @pl.when(step == steps - 1)
    def _():
        for t in range(n_ten):
            part[half, t] = acc[:, t * cols : (t + 1) * cols].astype(BF16)

    @pl.when((half == 0) & (step == steps - 1))
    def _():
        pl.semaphore_wait(pltpu.get_barrier_semaphore(), n_ten + n_rep - 2)
        for d in range(1, n_ten):
            to_ten(0, d).start()

    @pl.when((half == 1) & (step == 0))
    def _():
        route(0)

    @pl.when((half == 1) & (step == steps - 1))
    def _():
        for d in range(1, n_ten):
            to_ten(1, d).start()
        route(1)

        for copy in later:
            copy.wait()
        places = cache_ref.shape[1] * kvh
        col = lax.broadcasted_iota(jnp.int32, (heads, places), 1)
        row = lax.broadcasted_iota(jnp.int32, (heads, places), 0)
        same_head = lax.rem(col, kvh) == row // group
        for b in range(reqs):
            query = sq_ref[b]
            both = cache_ref[b].astype(F32).reshape(places, 2 * width).astype(BF16)
            score = (
                lax.dot_general(
                    query, both[:, :width], (((1,), (1,)), ((), ())), preferred_element_type=F32
                )
                * scale
            )
            live = same_head & (col // kvh < len_ref[b])
            weight = jnp.where(live, jnp.exp(score), 0.0)
            fresh = jnp.broadcast_to(
                fresh_ref[b].astype(F32)[:, None, :], (kvh, group, 2 * width)
            ).reshape(heads, 2 * width)
            fresh_weight = jnp.exp(
                jnp.sum(query.astype(F32) * fresh[:, :width], axis=1, keepdims=True) * scale
            )
            total = jnp.sum(weight, axis=1, keepdims=True) + fresh_weight
            numer = jnp.dot(
                weight.astype(BF16), both[:, width:], preferred_element_type=F32
            )
            numer = numer + fresh_weight.astype(BF16).astype(F32) * fresh[:, width:]
            self_ref[b] = (numer / total).astype(BF16)

        cross_query = cq_ref[...].astype(F32)
        size = n_rep * slot_rows
        owner_row = lax.broadcasted_iota(jnp.int32, (reqs * group, size), 0) // group
        mask = owner_row == code_ref[...]
        has = jnp.sum(mask.astype(F32), axis=1, keepdims=True) > 0.0
        for d in range(1, n_rep):
            wait_arrival(0, d)
        safe = []
        for h in range(kvh):
            query = cross_query[:, h * group : (h + 1) * group, :]
            query = query.reshape(reqs * group, width).astype(BF16)
            raw = arrived[0, :, :, h * width : (h + 1) * width].astype(F32).reshape(size, width)
            keys = (
                raw * lax.rsqrt(jnp.mean(raw * raw, axis=1, keepdims=True) + 1e-05)
            ).astype(BF16)
            score = (
                lax.dot_general(
                    query, keys, (((1,), (1,)), ((), ())), preferred_element_type=F32
                )
                * scale
            )
            weight = jnp.where(mask, jnp.exp(score), 0.0)
            safe.append(jnp.where(has, jnp.sum(weight, axis=1, keepdims=True), 1.0))
            weights[h] = weight.astype(BF16)
        for d in range(1, n_rep):
            wait_arrival(1, d)
        parts = []
        for h in range(kvh):
            values = arrived[1, :, :, h * width : (h + 1) * width]
            values = values.astype(F32).reshape(size, width).astype(BF16)
            numer = jnp.dot(weights[h], values, preferred_element_type=F32)
            parts.append(jnp.where(has, numer / safe[h], 0.0).reshape(reqs, group, width))
        cross_ref[...] = jnp.concatenate(parts, axis=1).astype(BF16)

        for which in range(2):
            for d in range(1, n_ten):
                to_ten(which, d).wait_send()
            for d in range(1, n_rep):
                to_rep(which, d).wait_send()


def local(
    n_rep,
    n_ten,
    features,
    kv_weight,
    image_owner,
    image_request,
    cross_query,
    self_query,
    self_cache,
    fresh_key_value,
    cache_len,
):
    images, patches, depth = features.shape
    reqs, heads, width = cross_query.shape
    kvh = self_cache.shape[2]
    kvh_all = kv_weight.shape[1]
    group = heads // kvh
    slot_cap = max(2, 2 * images // n_rep)
    rows = images * patches
    slot_rows = slot_cap * patches

    lanes = 128 // math.gcd(128, images) * images
    chunk = depth
    for c in range(256, 769, 256):
        if depth % c == 0:
            chunk = c
    steps = depth // chunk
    cols = kvh * width
    tile = 256 // kvh_all * kvh_all
    vmem = pl.BlockSpec(memory_space=pltpu.VMEM)
    hbm = pl.BlockSpec(memory_space=pltpu.HBM)
    return pl.pallas_call(
        functools.partial(step_kernel, n_rep, n_ten, kvh_all, kvh, slot_cap),
        grid=(2, steps),
        in_specs=[
            vmem,
            vmem,
            hbm,
            hbm,
            pl.BlockSpec((chunk * kvh_all, width), lambda j, k: (k, j)),
            hbm,
            hbm,
            hbm,
            hbm,
        ],
        out_specs=(vmem, vmem),
        out_shape=(
            jax.ShapeDtypeStruct(cross_query.shape, BF16),
            jax.ShapeDtypeStruct(self_query.shape, BF16),
        ),
        scratch_shapes=[
            pltpu.SMEM(cache_len.shape, jnp.int32),
            pltpu.VMEM((steps, images, patches, chunk), BF16),
            pltpu.VMEM(cross_query.shape, BF16),
            pltpu.VMEM(self_query.shape, BF16),
            pltpu.VMEM(self_cache.shape, BF16),
            pltpu.VMEM(fresh_key_value.shape, BF16),
            pltpu.VMEM((n_rep, images), jnp.int32),
            pltpu.VMEM((1, rows), jnp.int32),
            pltpu.VMEM((1, n_rep * slot_rows), jnp.int32),
            pltpu.VMEM((tile, tile), BF16),
            pltpu.VMEM((steps, rows, chunk), BF16),
            pltpu.VMEM((kvh_all // 2, chunk, 2 * width), BF16),
            pltpu.VMEM((rows, kvh_all * width), F32),
            pltpu.VMEM((2, n_ten, rows, cols), BF16),
            pltpu.VMEM((2, n_ten - 1, rows, cols), BF16),
            pltpu.VMEM((2, n_rep, slot_rows, cols), BF16),
            pltpu.VMEM((2, n_rep, slot_rows, cols), BF16),
            pltpu.VMEM((kvh, reqs * group, n_rep * slot_rows), BF16),
            pltpu.SemaphoreType.DMA((steps,)),
            pltpu.SemaphoreType.DMA((5,)),
            pltpu.SemaphoreType.DMA((2, n_ten - 1)),
            pltpu.SemaphoreType.DMA((2, n_ten - 1)),
            pltpu.SemaphoreType.DMA((2, n_rep)),
            pltpu.SemaphoreType.DMA((2, n_rep)),
        ],
        compiler_params=pltpu.CompilerParams(
            collective_id=0,
            has_side_effects=True,
            vmem_limit_bytes=60 * 1024 * 1024,
        ),
    )(
        image_owner.reshape(n_rep * images // lanes, lanes),
        image_request.reshape(n_rep * images // lanes, lanes),
        cache_len,
        features,
        kv_weight.reshape(depth * kvh_all, 2 * width),
        cross_query,
        self_query,
        self_cache,
        fresh_key_value,
    )


def solution(mesh):
    n_rep, n_ten = mesh.shape["replica"], mesh.shape["tensor"]
    return jax.shard_map(
        functools.partial(local, n_rep, n_ten),
        mesh=mesh,
        in_specs=(
            P("replica", None, "tensor"),
            P("tensor", None, None),
            P(),
            P(),
            P("replica", "tensor", None),
            P("replica", "tensor", None),
            P("replica", None, "tensor", None),
            P("replica", "tensor", None),
            P("replica"),
        ),
        out_specs=(P("replica", "tensor", None), P("replica", "tensor", None)),
        check_vma=False,
    )
```
